512 devices in a mesh: rows: 8 (over z_lo), chan: 64 (over y, x, z_hi, core).
Axes of the slice: x: 4, y: 4, z: 16 (z_hi: 2, z_lo: 8; z = z_hi * 8 + z_lo), core: 2. Of those that a mesh axis runs over, the one named last changes fastest.
Arguments:
- activations: bfloat16 [256, 7, 7, 512], P('rows', None, None, 'chan'), may hold values from 0 to 2
- cotangents: bfloat16 [256, 512, 49], P('rows', 'chan'), may hold values from -0.0005859375 to 0.0005859375
- ordering: int32 [8, 32], P('rows'), may hold values from 0 to 31, each once within a row
- ridge: float32 [128], replicated, may hold values from 0.2 to 2
Outputs:
- gram_panel: float32 [256, 128], P('rows')
- factor_panel: float32 [256, 128], P('rows')
The draws below stay inside these ranges and needn't reach their ends.
Inputs may be any that keep to these rules, and one draw needn't show every extreme that they name: Each row of ordering lists every one of the group's 32 examples once.
All inputs are finite; a program needn't handle non-finite values.
Results may differ from the reference program's by a relative error of at most 0.0003.
Values may be sent and summed in bfloat16 or wider, within the bound.
A program may use at most 64 MiB of HBM per device.

```python
import math
import jax
import jax.numpy as jnp
from jax import lax

CIN = 512
COUT = 512
SIDE = 7
ROW_DEV = 32
PIV_DEV = 16
HW = 49
GROUPS = 8
ROWS = 256
PIV = 128


def draw_cotangents(key, part):
    scale_base = 0.0413 / math.sqrt(COUT * CIN)
    shared = jax.random.uniform(jax.random.fold_in(key, 7), (COUT, HW), jnp.float32, -1.7, 1.7)
    own_part = jnp.clip(jax.random.normal(key, (ROWS, COUT, HW), jnp.float32), -1.7, 1.7)
    row_scale = jnp.ones((ROWS, 1, 1), jnp.float32)
    values = scale_base * row_scale * (0.6 * shared[None, :, :] + 0.8 * own_part)
    return values.astype(jnp.bfloat16)


def steps_of(own_key, extent, shards, smallest, high):
    factor_of, own = 1.0, jax.random.fold_in(own_key, 6)
    for dim, shards_of in shards:
        steps = jnp.exp(jax.random.uniform(jax.random.fold_in(own, dim), (shards_of,), jnp.float32, smallest / len(shards), high / len(shards)))
        factor_of = factor_of * jnp.repeat(steps, extent[dim] // shards_of).reshape([-1 if axis == dim else 1 for axis in range(len(extent))])
    return factor_of


def setup_inputs(seed: int = 0) -> dict:
    arg_keys = jax.random.split(jax.random.key(seed), 5)
    activations = jnp.clip(2.0 * jax.random.uniform(arg_keys[0], (ROWS, SIDE, SIDE, CIN), jnp.float32) ** steps_of(arg_keys[0], (ROWS, SIDE, SIDE, CIN), ((0, 8), (3, 64)), -0.2, 0.2), 0.0, 2.0).astype(jnp.bfloat16)
    cotangents = draw_cotangents(jax.random.fold_in(arg_keys[4], 71), 0)
    ordering = jax.vmap(lambda own: jax.random.permutation(own, ROW_DEV))(jax.random.split(arg_keys[2], GROUPS)).reshape((GROUPS, ROW_DEV)).astype(jnp.int32)
    ridge = jnp.clip(jnp.exp(jax.random.uniform(arg_keys[3], (PIV,), jnp.float32, math.log(0.2), math.log(2.0))), 0.2, 2.0)
    return {"activations": activations, "cotangents": cotangents, "ordering": ordering, "ridge": ridge}


def jacobian(grad_rows, input_rows):
    example_count = input_rows.shape[0]
    side_len = input_rows.shape[1]
    channel_count = input_rows.shape[3]
    padded = jnp.pad(input_rows.astype(jnp.float32), ((0, 0), (1, 1), (1, 1), (0, 0)))
    grads_wide = grad_rows.astype(jnp.float32)
    columns = []
    for row_shift in range(3):
        for col_shift in range(3):
            window = padded[:, row_shift:row_shift + side_len, col_shift:col_shift + side_len, :]
            window = window.reshape(example_count, side_len * side_len, channel_count)
            columns.append(jnp.einsum('ncp,npq->ncq', grads_wide, window))
    stacked = jnp.stack(columns, axis=2).astype(jnp.bfloat16)
    return stacked.reshape(example_count, -1)

def reference(activations, cotangents, ordering, ridge):
    bases = jnp.arange(GROUPS, dtype=jnp.int32)[:, None] * ROW_DEV
    row_index = (bases + ordering.astype(jnp.int32)).reshape(-1)
    pivot_index = (bases + jnp.arange(PIV_DEV, dtype=jnp.int32)[None, :]).reshape(-1)
    row_inputs = jnp.take(activations, row_index, axis=0)
    row_grads = jnp.take(cotangents, row_index, axis=0)
    pivot_inputs = jnp.take(row_inputs, pivot_index, axis=0)
    pivot_grads = jnp.take(row_grads, pivot_index, axis=0)
    block_width = 16 if COUT % 16 == 0 else COUT

    def accumulate(running, block_index):
        first_channel = (block_index * block_width).astype(jnp.int32)
        own_block = lax.dynamic_slice_in_dim(row_grads, first_channel, block_width, 1)
        pivot_block = lax.dynamic_slice_in_dim(pivot_grads, first_channel, block_width, 1)
        own_jac = jacobian(own_block, row_inputs)
        pivot_jac = jacobian(pivot_block, pivot_inputs)
        product = lax.dot_general(own_jac.astype(jnp.float32), pivot_jac.astype(jnp.float32), (((1,), (1,)), ((), ())), preferred_element_type=jnp.float32)
        return (running + product, None)
    gram_panel, _ = lax.scan(accumulate, jnp.zeros((ROWS, PIV), jnp.float32), jnp.arange(COUT // block_width, dtype=jnp.int32))
    diag_block = jnp.take(gram_panel, pivot_index, axis=0)
    system = 0.5 * (diag_block + diag_block.T) + jnp.diag(ridge)
    lower = jnp.linalg.cholesky(system)
    factor_panel = jax.scipy.linalg.solve_triangular(lower, gram_panel.T, lower=True).T
    return (gram_panel, factor_panel)
```

```python
import functools

import jax
import jax.numpy as jnp
from jax import lax
from jax.experimental import pallas as pl
from jax.experimental.pallas import tpu as pltpu
from jax.sharding import PartitionSpec as P

F32 = jnp.float32
BF16 = jnp.bfloat16
MESH = pl.DeviceIdType.MESH
VM = pl.BlockSpec(memory_space=pltpu.VMEM)
SM = pl.BlockSpec(memory_space=pltpu.SMEM)


def place():
    k = lax.axis_index("rows")
    j = lax.axis_index("chan")
    return k, j // 4, (j // 2) % 2, j % 2


def dev(k, yx, zh, c):
    return {"rows": k, "chan": (yx * 2 + zh) * 2 + c}


def plane_peer(a, i):
    other = (a + i) % 32
    return other // 2, other % 2


def z_dev(z, yx, c):
    z = z % 16
    return dev(z % 8, yx, z // 8, c)


def prep_kernel(order_ref, x_ref, g_ref, out_ref, ge, go, xs):
    _, _, _, c = place()
    pos = lax.broadcasted_iota(jnp.int32, (49, 128), 0)
    lane = lax.broadcasted_iota(jnp.int32, (49, 128), 1)
    slot = (pos // 7) * 8 + pos % 7
    low = jnp.where(lane == slot, 1.0, 0.0).astype(BF16)
    high = jnp.where(lane == slot + 64, 1.0, 0.0).astype(BF16)
    for u in range(16):
        ge[pl.ds(u * 8, 8), :] = g_ref[order_ref[0, 2 * u]].astype(F32)
        go[pl.ds(u * 8, 8), :] = g_ref[order_ref[0, 2 * u + 1]].astype(F32)
    grads = jnp.dot(ge[...].astype(BF16), low, preferred_element_type=F32) + jnp.dot(
        go[...].astype(BF16), high, preferred_element_type=F32
    )
    grads = grads.reshape(16, 8, 128)
    unit = lax.broadcasted_iota(jnp.int32, (16, 32), 0)
    example = lax.broadcasted_iota(jnp.int32, (16, 32), 1)
    even = jnp.zeros((16, 32), F32)
    odd = jnp.zeros((16, 32), F32)
    for u in range(16):
        even = jnp.where((unit == u) & (example == order_ref[0, 2 * u]), 1.0, even)
        odd = jnp.where((unit == u) & (example == order_ref[0, 2 * u + 1]), 1.0, odd)
    even = even.astype(BF16)
    odd = odd.astype(BF16)
    for ch in range(8):
        block = x_ref[:, ch, :]
        dims = (((0,), (0,)), ((), ()))
        at_low = lax.dot_general(block, low, dims, preferred_element_type=F32).astype(BF16)
        at_high = lax.dot_general(block, high, dims, preferred_element_type=F32).astype(BF16)
        xs[:, ch, :] = jnp.dot(even, at_low, preferred_element_type=F32) + jnp.dot(
            odd, at_high, preferred_element_type=F32
        )
    inputs = xs[...]
    first = jnp.where(c == 0, grads, inputs)
    second = jnp.where(c == 0, inputs, grads)
    out_ref[...] = jnp.concatenate([first, second], axis=1).astype(BF16)


def prep(order, x, g):
    return pl.pallas_call(
        prep_kernel,
        out_shape=jax.ShapeDtypeStruct((16, 16, 128), BF16),
        in_specs=[SM, VM, VM],
        out_specs=VM,
        scratch_shapes=[
            pltpu.VMEM((128, 49), F32),
            pltpu.VMEM((128, 49), F32),
            pltpu.VMEM((16, 8, 128), F32),
        ],
        name="prep",
    )(order, x, g)


def gather_kernel(t_ref, rows_ref, piv_ref, mate_ref, mate_sem, row_send, row_recv, a2a_send, a2a_recv,
                  ring_send, ring_recv, sib_send, sib_recv):
    k, yx, zh, c = place()
    z = zh * 8 + k
    a = yx * 2 + c
    par = yx % 2
    away = (k + par) % 2
    slot_of = (zh * 2 + c) * 16 + yx
    mate_slot = ((1 - zh) * 2 + c) * 16 + yx
    mate_dev = dev(k, yx, 1 - zh, c)
    sib_dev = dev(k, yx, zh, 1 - c)

    barrier = pltpu.get_barrier_semaphore()

    @pl.loop(1, 32)
    def _(i):
        yx2, c2 = plane_peer(a, i)
        pl.semaphore_signal(barrier, inc=1, device_id=dev(k, yx2, zh, c2), device_id_type=MESH)

    for other in (mate_dev, z_dev(z + 1, yx, c), z_dev(z + 15, yx, c)):
        pl.semaphore_signal(barrier, inc=1, device_id=other, device_id_type=MESH)
    pl.semaphore_wait(barrier, 34)

    to_mate = pltpu.make_async_remote_copy(
        src_ref=t_ref.at[pl.ds(8 * (1 - zh), 8)], dst_ref=mate_ref,
        send_sem=mate_sem.at[0], recv_sem=mate_sem.at[1], device_id=mate_dev, device_id_type=MESH)
    to_mate.start()

    own_chunk = ((k // 2) * 2 + zh) * 2 + c
    for u in range(8):
        target = (u // 2) * 4 + 2 * (u % 2) + k % 2

        @pl.when(target == yx)
        def _():
            pltpu.make_async_copy(t_ref.at[u], piv_ref.at[own_chunk, yx], a2a_recv.at[0]).start()

        @pl.when(target != yx)
        def _():
            pltpu.make_async_remote_copy(
                src_ref=t_ref.at[u], dst_ref=piv_ref.at[own_chunk, yx],
                send_sem=a2a_send.at[0], recv_sem=a2a_recv.at[0],
                device_id=dev(k, target, zh, c), device_id_type=MESH).start()

    def send_rows(src_ref, base, slot):
        @pl.loop(1, 32)
        def _(i):
            yx2, c2 = plane_peer(a, i)
            pltpu.make_async_remote_copy(
                src_ref=src_ref.at[pl.ds(base + 4 * c2, 4)], dst_ref=rows_ref.at[slot],
                send_sem=row_send.at[0], recv_sem=row_recv.at[0],
                device_id=dev(k, yx2, zh, c2), device_id_type=MESH).start()

        pltpu.make_async_copy(src_ref.at[pl.ds(base + 4 * c, 4)], rows_ref.at[slot], row_recv.at[0]).start()

    def ring_copy(chunk, right, slot_send, slot_recv):
        way = 0 if right else 1
        target = z_dev(z + 1, yx, c) if right else z_dev(z + 15, yx, c)
        return pltpu.make_async_remote_copy(
            src_ref=piv_ref.at[chunk], dst_ref=piv_ref.at[chunk],
            send_sem=ring_send.at[way, slot_send], recv_sem=ring_recv.at[way, slot_recv],
            device_id=target, device_id_type=MESH)

    def sib_copy(chunk):
        return pltpu.make_async_remote_copy(
            src_ref=piv_ref.at[chunk], dst_ref=piv_ref.at[chunk],
            send_sem=sib_send.at[0], recv_sem=sib_recv.at[0],
            device_id=sib_dev, device_id_type=MESH)

    send_rows(t_ref, 8 * zh, slot_of)

    @pl.when(away == 0)
    def _():
        pltpu.make_async_copy(piv_ref.at[own_chunk], piv_ref.at[own_chunk], a2a_recv.at[0]).wait()
        ring_copy(own_chunk, True, 4, 0).start()
        ring_copy(own_chunk, False, 4, 0).start()
        sib_copy(own_chunk).start()

    to_mate.wait_recv()
    send_rows(mate_ref, 0, mate_slot)

    for n in range(4):
        dist = 2 * n + 2 - away
        for right in (True, False):
            src_z = (z + 16 - dist) % 16 if right else (z + dist) % 16
            chunk = (((src_z % 8) // 2) * 2 + src_z // 8) * 2 + c

            def arrive(right=right, chunk=chunk, n=n):
                ring_copy(chunk, right, n, n).wait_recv()

            def forward(right=right, chunk=chunk, n=n):
                ring_copy(chunk, right, n, n + 1 - away).start()

            if n < 3:
                arrive()
                forward()
                sib_copy(chunk).start()
            elif right:
                arrive()

                @pl.when(away == 1)
                def _():
                    forward()

                sib_copy(chunk).start()
            else:

                @pl.when(away == 1)
                def _():
                    arrive()
                    sib_copy(chunk).start()

    to_mate.wait_send()

    @pl.when(away == 0)
    def _():
        pltpu.make_async_copy(t_ref.at[pl.ds(0, 7)], t_ref.at[pl.ds(0, 7)], a2a_send.at[0]).wait()
        for right in (True, False):
            ring_copy(own_chunk, right, 4, 0).wait_send()
            for n in range(3):
                ring_copy(own_chunk, right, n, 0).wait_send()

    @pl.when(away == 1)
    def _():
        pltpu.make_async_copy(t_ref.at[pl.ds(0, 8)], t_ref.at[pl.ds(0, 8)], a2a_send.at[0]).wait()
        for n in range(4):
            ring_copy(own_chunk, True, n, 0).wait_send()
        for n in range(3):
            ring_copy(own_chunk, False, n, 0).wait_send()

    pltpu.make_async_copy(rows_ref.at[pl.ds(0, 62)], rows_ref.at[pl.ds(0, 62)], row_send.at[0]).wait()
    pltpu.make_async_copy(rows_ref, rows_ref, row_recv.at[0]).wait()
    pltpu.make_async_copy(piv_ref.at[pl.ds(0, 8)], piv_ref.at[pl.ds(0, 8)], sib_send.at[0]).wait()
    pltpu.make_async_copy(piv_ref.at[pl.ds(0, 8)], piv_ref.at[pl.ds(0, 8)], sib_recv.at[0]).wait()


def gather(t):
    return pl.pallas_call(
        gather_kernel,
        out_shape=[
            jax.ShapeDtypeStruct((64, 4, 16, 128), BF16),
            jax.ShapeDtypeStruct((16, 16, 16, 128), BF16),
        ],
        in_specs=[VM],
        out_specs=[VM, VM],
        scratch_shapes=[
            pltpu.VMEM((8, 16, 128), BF16),
            pltpu.SemaphoreType.DMA((2,)),
            pltpu.SemaphoreType.DMA((1,)),
            pltpu.SemaphoreType.DMA((1,)),
            pltpu.SemaphoreType.DMA((1,)),
            pltpu.SemaphoreType.DMA((1,)),
            pltpu.SemaphoreType.DMA((2, 5)),
            pltpu.SemaphoreType.DMA((2, 4)),
            pltpu.SemaphoreType.DMA((1,)),
            pltpu.SemaphoreType.DMA((1,)),
        ],
        compiler_params=pltpu.CompilerParams(
            collective_id=0, has_side_effects=True, vmem_limit_bytes=16 * 1024 * 1024),
        name="gather_inputs",
    )(t)


def block_kernel(rows_ref, piv_ref, out_ref, ag, ax, bg, bx, gg, xx):
    k, yx, zh, c = place()
    mask = lax.broadcasted_iota(jnp.int32, (16, 16, 128), 1) < 8

    for z2 in range(2):
        for u in range(4):
            even = rows_ref[pl.ds(z2 * 32, 16), u]
            odd = rows_ref[pl.ds(z2 * 32 + 16, 16), u]
            ag[pl.ds(z2 * 256, 256), pl.ds(u * 128, 128)] = jnp.where(mask, even, odd).reshape(256, 128)
            ax[pl.ds(z2 * 256, 256), pl.ds(u * 128, 128)] = jnp.where(mask, odd, even).reshape(256, 128)
            even = piv_ref[(u * 2 + z2) * 2]
            odd = piv_ref[(u * 2 + z2) * 2 + 1]
            bg[pl.ds(z2 * 256, 256), pl.ds(u * 128, 128)] = jnp.where(mask, even, odd).reshape(256, 128)
            bx[pl.ds(z2 * 256, 256), pl.ds(u * 128, 128)] = jnp.where(mask, odd, even).reshape(256, 128)
    dims = (((0,), (0,)), ((), ()))
    gg[...] = lax.dot_general(ag[...], bg[...], dims, preferred_element_type=F32)
    xx[...] = lax.dot_general(ax[...], bx[...], dims, preferred_element_type=F32)
    lanes = lax.broadcasted_iota(jnp.int32, (128, 128), 0)
    cols = lax.broadcasted_iota(jnp.int32, (128, 128), 1)
    piv0 = 16 * (yx % 2) + 2 * ((yx // 4) * 2 + (yx % 4) // 2)
    pieces = jnp.zeros((8, 128), F32)
    for t in range(4):
        col = pl.ds(t * 128, 128)
        summed = []
        for e in range(8):
            wide = xx[pl.ds(e * 64, 64), col]
            wide = (
                wide
                + pltpu.roll(pltpu.roll(wide, 1, 0), 1, 1)
                + pltpu.roll(pltpu.roll(wide, 63, 0), 127, 1)
            )
            wide = (
                wide
                + pltpu.roll(pltpu.roll(wide, 8, 0), 8, 1)
                + pltpu.roll(pltpu.roll(wide, 56, 0), 120, 1)
            )
            summed.append(jnp.sum(gg[pl.ds(e * 64, 64), col] * wide, axis=0, keepdims=True))
        folded = jnp.concatenate(summed, axis=0)
        spread = jnp.where(cols == piv0 + 32 * t + lanes // 64, 1.0, 0.0)
        pieces = pieces + jnp.dot(folded, spread, precision=lax.Precision.HIGHEST, preferred_element_type=F32)
    out_ref[...] = pieces


def block(rows, piv):
    return pl.pallas_call(
        block_kernel,
        out_shape=jax.ShapeDtypeStruct((8, 128), F32),
        in_specs=[VM, VM],
        out_specs=VM,
        scratch_shapes=[pltpu.VMEM((512, 512), BF16)] * 4 + [pltpu.VMEM((512, 512), F32)] * 2,
        compiler_params=pltpu.CompilerParams(vmem_limit_bytes=24 * 1024 * 1024),
        name="kernel_block",
    )(rows, piv)


def panel_kernel(part_ref, diag_ref, rest_ref, parts, plane_rows, send1, recv1, send2, recv2, recv3):
    k, yx, zh, c = place()
    z = zh * 8 + k
    a = yx * 2 + c
    barrier = pltpu.get_barrier_semaphore()

    @pl.loop(1, 32)
    def _(i):
        yx2, c2 = plane_peer(a, i)
        pl.semaphore_signal(barrier, inc=1, device_id=dev(k, yx2, zh, c2), device_id_type=MESH)

    @pl.loop(1, 16)
    def _(i):
        pl.semaphore_signal(barrier, inc=1, device_id=z_dev(z + i, yx, c), device_id_type=MESH)

    pl.semaphore_wait(barrier, 46)

    slot = c * 16 + yx

    @pl.loop(1, 32)
    def _(i):
        yx2, c2 = plane_peer(a, i)
        pltpu.make_async_remote_copy(
            src_ref=part_ref, dst_ref=parts.at[slot], send_sem=send1.at[0], recv_sem=recv1.at[0],
            device_id=dev(k, yx2, zh, c2), device_id_type=MESH).start()

    pltpu.make_async_copy(part_ref, parts.at[slot], recv1.at[0]).start()
    pltpu.make_async_copy(parts, parts, recv1.at[0]).wait()
    for c2 in range(2):
        plane_rows[pl.ds(c2 * 8, 8), :] = jnp.sum(parts[pl.ds(c2 * 16, 16)], axis=0)

    @pl.when(zh == 0)
    def _():
        @pl.loop(1, 16)
        def _(i):
            pltpu.make_async_remote_copy(
                src_ref=plane_rows, dst_ref=diag_ref.at[k], send_sem=send2.at[0], recv_sem=recv2.at[0],
                device_id=z_dev(z + i, yx, c), device_id_type=MESH).start()

        pltpu.make_async_copy(plane_rows, diag_ref.at[k], recv2.at[0]).start()

    @pl.when(zh == 1)
    def _():
        pltpu.make_async_remote_copy(
            src_ref=plane_rows, dst_ref=rest_ref, send_sem=send2.at[0], recv_sem=recv3.at[0],
            device_id=dev(k, yx, 0, c), device_id_type=MESH).start()
        pltpu.make_async_copy(plane_rows, rest_ref, recv3.at[0]).start()

    pltpu.make_async_copy(diag_ref, diag_ref, recv2.at[0]).wait()
    pltpu.make_async_copy(rest_ref, rest_ref, recv3.at[0]).wait()
    pltpu.make_async_copy(parts.at[pl.ds(0, 31)], parts.at[pl.ds(0, 31)], send1.at[0]).wait()

    @pl.when(zh == 0)
    def _():
        pltpu.make_async_copy(parts.at[pl.ds(0, 30)], parts.at[pl.ds(0, 30)], send2.at[0]).wait()

    @pl.when(zh == 1)
    def _():
        pltpu.make_async_copy(plane_rows, plane_rows, send2.at[0]).wait()


def panel(part):
    return pl.pallas_call(
        panel_kernel,
        out_shape=[jax.ShapeDtypeStruct((8, 16, 128), F32), jax.ShapeDtypeStruct((16, 128), F32)],
        in_specs=[VM],
        out_specs=[VM, VM],
        scratch_shapes=[
            pltpu.VMEM((32, 8, 128), F32),
            pltpu.VMEM((16, 128), F32),
        ] + [pltpu.SemaphoreType.DMA((1,))] * 5,
        compiler_params=pltpu.CompilerParams(collective_id=1, has_side_effects=True),
        name="gather_panel",
    )(part)


def solve_kernel(diag_ref, rest_ref, ridge_ref, gram_ref, factor_ref):
    k, _, _, _ = place()
    gram_ref[pl.ds(0, 16), :] = diag_ref[k]
    gram_ref[pl.ds(16, 16), :] = rest_ref[...]
    gram = gram_ref[...]
    diag = diag_ref[...].reshape(128, 128)
    row = lax.broadcasted_iota(jnp.int32, (128, 128), 0)
    col = lax.broadcasted_iota(jnp.int32, (128, 128), 1)
    system = 0.5 * (diag + diag.T) + jnp.where(row == col, ridge_ref[...], 0.0)
    right = jnp.concatenate([gram, jnp.zeros((96, 128), F32)], axis=0).T
    sub = lax.broadcasted_iota(jnp.int32, (8, 128), 0)
    left = [system[8 * m:8 * m + 8] for m in range(16)]
    right = [right[8 * m:8 * m + 8] for m in range(16)]
    for j in range(128):
        m0, i = j // 8, j % 8
        pivot_row = left[m0][i:i + 1, :]
        right_row = right[m0][i:i + 1, :]
        pivot = left[m0][i:i + 1, j:j + 1]
        inverse = 1.0 / pivot
        scaled_row = pivot_row * inverse
        scaled_right = right_row * inverse
        for m in range(m0, 16):
            factor = jnp.broadcast_to(left[m][:, j:j + 1], (8, 128))
            if m == m0:
                factor = jnp.where(sub > i, factor, 0.0)
            left[m] = left[m] - factor * scaled_row
            right[m] = right[m] - factor * scaled_right
    lane = lax.broadcasted_iota(jnp.int32, (8, 128), 1)
    for m in range(16):
        pivots = jnp.sum(jnp.where(lane == sub + 8 * m, left[m], 0.0), axis=1, keepdims=True)
        right[m] = right[m] * lax.rsqrt(pivots)
    factor_ref[...] = jnp.concatenate(right, axis=0).T[:32]


def solve(diag, rest, ridge):
    out = jax.ShapeDtypeStruct((32, 128), F32)
    return pl.pallas_call(
        solve_kernel,
        out_shape=[out, out],
        in_specs=[VM, VM, VM],
        out_specs=[VM, VM],
        name="factor_solve",
    )(diag, rest, ridge)


def local(activations, cotangents, ordering, ridge):
    x = activations.transpose(1, 2, 3, 0).reshape(49, 8, 32)
    t = prep(ordering, x, cotangents)
    rows, piv = gather(t)
    part = block(rows, piv)
    diag, rest = panel(part)
    return tuple(solve(diag, rest, ridge.reshape(1, 128)))


def solution(mesh):
    return jax.shard_map(
        local,
        mesh=mesh,
        in_specs=(P("rows", None, None, "chan"), P("rows", "chan", None), P("rows", None), P()),
        out_specs=(P("rows", None), P("rows", None)),
        check_vma=False,
    )
```

```python
import functools

import jax
import jax.numpy as jnp
from jax import lax
from jax.experimental import pallas as pl
from jax.experimental.pallas import tpu as pltpu
from jax.sharding import PartitionSpec as P

F32 = jnp.float32
BF16 = jnp.bfloat16
MESH = pl.DeviceIdType.MESH
VM = pl.BlockSpec(memory_space=pltpu.VMEM)
SM = pl.BlockSpec(memory_space=pltpu.SMEM)


def place():
    k = lax.axis_index("rows")
    j = lax.axis_index("chan")
    return k, j // 4, (j // 2) % 2, j % 2


def dev(k, yx, zh, c):
    return {"rows": k, "chan": (yx * 2 + zh) * 2 + c}


def plane_peer(a, i):
    other = (a + i) % 32
    return other // 2, other % 2


def z_dev(z, yx, c):
    z = z % 16
    return dev(z % 8, yx, z // 8, c)


def lay_out(order_ref, x_ref, g_ref, out_ref, ge, go, xs, c):
    pos = lax.broadcasted_iota(jnp.int32, (49, 128), 0)
    lane = lax.broadcasted_iota(jnp.int32, (49, 128), 1)
    slot = (pos // 7) * 8 + pos % 7
    low = jnp.where(lane == slot, 1.0, 0.0).astype(BF16)
    high = jnp.where(lane == slot + 64, 1.0, 0.0).astype(BF16)
    for u in range(16):
        ge[pl.ds(u * 8, 8), :] = g_ref[order_ref[0, 2 * u]].astype(F32)
        go[pl.ds(u * 8, 8), :] = g_ref[order_ref[0, 2 * u + 1]].astype(F32)
    grads = jnp.dot(ge[...].astype(BF16), low, preferred_element_type=F32) + jnp.dot(
        go[...].astype(BF16), high, preferred_element_type=F32
    )
    grads = grads.reshape(16, 8, 128)
    unit = lax.broadcasted_iota(jnp.int32, (16, 32), 0)
    example = lax.broadcasted_iota(jnp.int32, (16, 32), 1)
    even = jnp.zeros((16, 32), F32)
    odd = jnp.zeros((16, 32), F32)
    for u in range(16):
        even = jnp.where((unit == u) & (example == order_ref[0, 2 * u]), 1.0, even)
        odd = jnp.where((unit == u) & (example == order_ref[0, 2 * u + 1]), 1.0, odd)
    even = even.astype(BF16)
    odd = odd.astype(BF16)
    for ch in range(8):
        part = x_ref[:, ch, :]
        dims = (((0,), (0,)), ((), ()))
        at_low = lax.dot_general(part, low, dims, preferred_element_type=F32).astype(BF16)
        at_high = lax.dot_general(part, high, dims, preferred_element_type=F32).astype(BF16)
        xs[:, ch, :] = jnp.dot(even, at_low, preferred_element_type=F32) + jnp.dot(
            odd, at_high, preferred_element_type=F32
        )
    inputs = xs[...]
    first = jnp.where(c == 0, grads, inputs)
    second = jnp.where(c == 0, inputs, grads)
    out_ref[...] = jnp.concatenate([first, second], axis=1).astype(BF16)


def block(rows_ref, piv_ref, out_ref, ag, ax, bg, bx, gg, xx, yx):
    mask = lax.broadcasted_iota(jnp.int32, (16, 16, 128), 1) < 8
    for z2 in range(2):
        for u in range(4):
            even = rows_ref[pl.ds(z2 * 32, 16), u]
            odd = rows_ref[pl.ds(z2 * 32 + 16, 16), u]
            ag[pl.ds(z2 * 256, 256), pl.ds(u * 128, 128)] = jnp.where(mask, even, odd).reshape(256, 128)
            ax[pl.ds(z2 * 256, 256), pl.ds(u * 128, 128)] = jnp.where(mask, odd, even).reshape(256, 128)
            even = piv_ref[(u * 2 + z2) * 2]
            odd = piv_ref[(u * 2 + z2) * 2 + 1]
            bg[pl.ds(z2 * 256, 256), pl.ds(u * 128, 128)] = jnp.where(mask, even, odd).reshape(256, 128)
            bx[pl.ds(z2 * 256, 256), pl.ds(u * 128, 128)] = jnp.where(mask, odd, even).reshape(256, 128)
    dims = (((0,), (0,)), ((), ()))
    gg[...] = lax.dot_general(ag[...], bg[...], dims, preferred_element_type=F32)
    xx[...] = lax.dot_general(ax[...], bx[...], dims, preferred_element_type=F32)
    lanes = lax.broadcasted_iota(jnp.int32, (128, 128), 0)
    cols = lax.broadcasted_iota(jnp.int32, (128, 128), 1)
    piv0 = 16 * (yx % 2) + 2 * ((yx // 4) * 2 + (yx % 4) // 2)
    pieces = jnp.zeros((8, 128), F32)
    for t in range(4):
        col = pl.ds(t * 128, 128)
        summed = []
        for e in range(8):
            wide = xx[pl.ds(e * 64, 64), col]
            wide = (
                wide
                + pltpu.roll(pltpu.roll(wide, 1, 0), 1, 1)
                + pltpu.roll(pltpu.roll(wide, 63, 0), 127, 1)
            )
            wide = (
                wide
                + pltpu.roll(pltpu.roll(wide, 8, 0), 8, 1)
                + pltpu.roll(pltpu.roll(wide, 56, 0), 120, 1)
            )
            summed.append(jnp.sum(gg[pl.ds(e * 64, 64), col] * wide, axis=0, keepdims=True))
        folded = jnp.concatenate(summed, axis=0)
        spread = jnp.where(cols == piv0 + 32 * t + lanes // 64, 1.0, 0.0)
        pieces = pieces + jnp.dot(folded, spread, precision=lax.Precision.HIGHEST, preferred_element_type=F32)
    out_ref[...] = pieces


def panel_kernel(order_ref, x_ref, g_ref, diag_ref, rest_ref,
                 ge, go, xs, t_ref, mate_ref, rows_ref, piv_ref, ag, ax, bg, bx, gg, xx, part_ref, parts, plane_rows,
                 mate_sem, row_send, row_recv, a2a_send, a2a_recv, hub_send, hub_recv, near_send, near_recv,
                 sib_send, sib_recv, send1, recv1, send2, recv2, recv3):
    k, yx, zh, c = place()
    z = zh * 8 + k
    a = yx * 2 + c
    away = (k + yx) % 2
    mate_dev = dev(k, yx, 1 - zh, c)
    sib_dev = dev(k, yx, zh, 1 - c)

    barrier = pltpu.get_barrier_semaphore()

    @pl.loop(1, 32)
    def _(i):
        yx2, c2 = plane_peer(a, i)
        pl.semaphore_signal(barrier, inc=1, device_id=dev(k, yx2, zh, c2), device_id_type=MESH)

    @pl.loop(1, 16)
    def _(i):
        pl.semaphore_signal(barrier, inc=1, device_id=z_dev(z + i, yx, c), device_id_type=MESH)

    lay_out(order_ref, x_ref, g_ref, t_ref, ge, go, xs, c)
    pl.semaphore_wait(barrier, 46)

    def remote(src, dst, send, recv, target):
        return pltpu.make_async_remote_copy(
            src_ref=src, dst_ref=dst, send_sem=send, recv_sem=recv, device_id=target, device_id_type=MESH)

    def drain(ref, sem):
        pltpu.make_async_copy(ref, ref, sem).wait()

    to_mate = remote(t_ref.at[pl.ds(8 * (1 - zh), 8)], mate_ref, mate_sem.at[0], mate_sem.at[1], mate_dev)
    to_mate.start()

    def chunk_of(src_z):
        src_z = (src_z + 32) % 16
        return (((src_z % 8) // 2) * 2 + src_z // 8) * 2 + c

    own_chunk = chunk_of(z)
    for u in range(8):
        target = (u // 2) * 4 + 2 * (u % 2) + k % 2

        @pl.when(target == yx)
        def _():
            pltpu.make_async_copy(t_ref.at[u], piv_ref.at[own_chunk, yx], a2a_recv.at[0]).start()

        @pl.when(target != yx)
        def _():
            remote(t_ref.at[u], piv_ref.at[own_chunk, yx], a2a_send.at[0], a2a_recv.at[0],
                   dev(k, target, zh, c)).start()

    def send_rows(src_ref, base, slot):
        @pl.loop(1, 32)
        def _(i):
            yx2, c2 = plane_peer(a, i)
            remote(src_ref.at[pl.ds(base + 4 * c2, 4)], rows_ref.at[slot], row_send.at[0], row_recv.at[0],
                   dev(k, yx2, zh, c2)).start()

        pltpu.make_async_copy(src_ref.at[pl.ds(base + 4 * c, 4)], rows_ref.at[slot], row_recv.at[0]).start()

    def piv_copy(chunk, target, send, recv):
        return remote(piv_ref.at[chunk], piv_ref.at[chunk], send, recv, target)

    def sib_copy(chunk):
        return piv_copy(chunk, sib_dev, sib_send.at[0], sib_recv.at[0])

    hub = (0, -4, 4, 8)

    def near(role, step, n, recv):
        return piv_copy(chunk_of(z + hub[role]), z_dev(z + 16 + step, yx, c), near_send.at[n], near_recv.at[recv])

    nears = [(0, 1, 0), (0, -1, 4), (0, 2, 0), (0, -2, 2),
             (1, 1, 1), (1, -1, 5), (1, 2, 1),
             (2, 1, 2), (2, -1, 6), (2, -2, 3),
             (3, 1, 3), (3, -1, 7)]

    def from_hub(role):
        for n, (r, step, recv) in enumerate(nears):
            if r == role:
                near(r, step, n, recv).start()
        sib_copy(chunk_of(z + hub[role])).start()

    send_rows(t_ref, 8 * zh, (zh * 2 + c) * 16 + yx)

    @pl.when(away == 0)
    def _():
        drain(piv_ref.at[own_chunk], a2a_recv.at[0])
        for role in (1, 2, 3):
            piv_copy(own_chunk, z_dev(z + 16 - hub[role], yx, c), hub_send.at[role - 1], hub_recv.at[role - 1]).start()
        from_hub(0)
        for role in (1, 2):
            piv_copy(own_chunk, sib_dev, hub_send.at[role - 1], hub_recv.at[role - 1]).wait_recv()
            from_hub(role)

    to_mate.wait_recv()
    send_rows(mate_ref, 0, ((1 - zh) * 2 + c) * 16 + yx)

    @pl.when(away == 0)
    def _():
        piv_copy(own_chunk, sib_dev, hub_send.at[2], hub_recv.at[2]).wait_recv()
        from_hub(3)
        for recv, src in enumerate((-2, -6, 2, 6)):
            piv_copy(own_chunk, sib_dev, near_send.at[0], near_recv.at[recv]).wait_recv()
            sib_copy(chunk_of(z + src)).start()

    @pl.when(away == 1)
    def _():
        for role in range(4):
            for side in range(2):
                step = 1 - 2 * side
                piv_copy(own_chunk, sib_dev, near_send.at[0], near_recv.at[4 * side + role]).wait_recv()
                sib_copy(chunk_of(z - step + hub[role])).start()

    to_mate.wait_send()

    @pl.when(away == 0)
    def _():
        drain(t_ref.at[pl.ds(0, 7)], a2a_send.at[0])
        for role in (1, 2, 3):
            piv_copy(own_chunk, sib_dev, hub_send.at[role - 1], hub_recv.at[role - 1]).wait_send()
        for n in range(len(nears)):
            piv_copy(own_chunk, sib_dev, near_send.at[n], near_recv.at[0]).wait_send()

    @pl.when(away == 1)
    def _():
        drain(t_ref.at[pl.ds(0, 8)], a2a_send.at[0])

    drain(rows_ref.at[pl.ds(0, 62)], row_send.at[0])
    drain(piv_ref.at[pl.ds(0, 8)], sib_send.at[0])
    drain(rows_ref, row_recv.at[0])
    drain(piv_ref.at[pl.ds(0, 8)], sib_recv.at[0])

    block(rows_ref, piv_ref, part_ref, ag, ax, bg, bx, gg, xx, yx)

    slot = c * 16 + yx

    @pl.loop(1, 32)
    def _(i):
        yx2, c2 = plane_peer(a, i)
        remote(part_ref, parts.at[slot], send1.at[0], recv1.at[0], dev(k, yx2, zh, c2)).start()

    pltpu.make_async_copy(part_ref, parts.at[slot], recv1.at[0]).start()
    drain(parts, recv1.at[0])
    for c2 in range(2):
        plane_rows[pl.ds(c2 * 8, 8), :] = jnp.sum(parts[pl.ds(c2 * 16, 16)], axis=0)

    @pl.when(zh == 0)
    def _():
        @pl.loop(1, 16)
        def _(i):
            remote(plane_rows, diag_ref.at[k], send2.at[0], recv2.at[0], z_dev(z + i, yx, c)).start()

        pltpu.make_async_copy(plane_rows, diag_ref.at[k], recv2.at[0]).start()

    @pl.when(zh == 1)
    def _():
        remote(plane_rows, rest_ref, send2.at[0], recv3.at[0], mate_dev).start()
        pltpu.make_async_copy(plane_rows, rest_ref, recv3.at[0]).start()

    drain(diag_ref, recv2.at[0])
    drain(rest_ref, recv3.at[0])
    drain(parts.at[pl.ds(0, 31)], send1.at[0])

    @pl.when(zh == 0)
    def _():
        drain(parts.at[pl.ds(0, 30)], send2.at[0])

    @pl.when(zh == 1)
    def _():
        drain(plane_rows, send2.at[0])


def panel(order, x, g):
    dma = pltpu.SemaphoreType.DMA
    return pl.pallas_call(
        panel_kernel,
        out_shape=[jax.ShapeDtypeStruct((8, 16, 128), F32), jax.ShapeDtypeStruct((16, 128), F32)],
        in_specs=[SM, VM, VM],
        out_specs=[VM, VM],
        scratch_shapes=[
            pltpu.VMEM((128, 49), F32),
            pltpu.VMEM((128, 49), F32),
            pltpu.VMEM((16, 8, 128), F32),
            pltpu.VMEM((16, 16, 128), BF16),
            pltpu.VMEM((8, 16, 128), BF16),
            pltpu.VMEM((64, 4, 16, 128), BF16),
            pltpu.VMEM((16, 16, 16, 128), BF16),
        ]
        + [pltpu.VMEM((512, 512), BF16)] * 4
        + [pltpu.VMEM((512, 512), F32)] * 2
        + [pltpu.VMEM((8, 128), F32), pltpu.VMEM((32, 8, 128), F32), pltpu.VMEM((16, 128), F32)]
        + [dma((n,)) for n in (2, 1, 1, 1, 1, 3, 3, 12, 8, 1, 1, 1, 1, 1, 1, 1)],
        compiler_params=pltpu.CompilerParams(
            collective_id=0, has_side_effects=True, vmem_limit_bytes=32 * 1024 * 1024),
        name="panel",
    )(order, x, g)


def solve_kernel(diag_ref, rest_ref, ridge_ref, gram_ref, factor_ref):
    k, _, _, _ = place()
    gram_ref[pl.ds(0, 16), :] = diag_ref[k]
    gram_ref[pl.ds(16, 16), :] = rest_ref[...]
    gram = gram_ref[...]
    diag = diag_ref[...].reshape(128, 128)
    row = lax.broadcasted_iota(jnp.int32, (128, 128), 0)
    col = lax.broadcasted_iota(jnp.int32, (128, 128), 1)
    system = 0.5 * (diag + diag.T) + jnp.where(row == col, ridge_ref[...], 0.0)
    right = jnp.concatenate([gram, jnp.zeros((96, 128), F32)], axis=0).T
    sub = lax.broadcasted_iota(jnp.int32, (8, 128), 0)
    left = [system[8 * m:8 * m + 8] for m in range(16)]
    right = [right[8 * m:8 * m + 8] for m in range(16)]
    for j in range(128):
        m0, i = j // 8, j % 8
        pivot_row = left[m0][i:i + 1, :]
        right_row = right[m0][i:i + 1, :]
        pivot = left[m0][i:i + 1, j:j + 1]
        inverse = 1.0 / pivot
        scaled_row = pivot_row * inverse
        scaled_right = right_row * inverse
        for m in range(m0, 16):
            factor = jnp.broadcast_to(left[m][:, j:j + 1], (8, 128))
            if m == m0:
                factor = jnp.where(sub > i, factor, 0.0)
            left[m] = left[m] - factor * scaled_row
            right[m] = right[m] - factor * scaled_right
    lane = lax.broadcasted_iota(jnp.int32, (8, 128), 1)
    for m in range(16):
        pivots = jnp.sum(jnp.where(lane == sub + 8 * m, left[m], 0.0), axis=1, keepdims=True)
        right[m] = right[m] * lax.rsqrt(pivots)
    factor_ref[...] = jnp.concatenate(right, axis=0).T[:32]


def solve(diag, rest, ridge):
    out = jax.ShapeDtypeStruct((32, 128), F32)
    return pl.pallas_call(
        solve_kernel,
        out_shape=[out, out],
        in_specs=[VM, VM, VM],
        out_specs=[VM, VM],
        name="factor_solve",
    )(diag, rest, ridge)


def local(activations, cotangents, ordering, ridge):
    x = activations.transpose(1, 2, 3, 0).reshape(49, 8, 32)
    diag, rest = panel(ordering, x, cotangents)
    return tuple(solve(diag, rest, ridge.reshape(1, 128)))


def solution(mesh):
    return jax.shard_map(
        local,
        mesh=mesh,
        in_specs=(P("rows", None, None, "chan"), P("rows", "chan", None), P("rows", None), P()),
        out_specs=(P("rows", None), P("rows", None)),
        check_vma=False,
    )
```

```python
import jax
import jax.numpy as jnp
from jax import lax
from jax.experimental import pallas as pl
from jax.experimental.pallas import tpu as pltpu
from jax.sharding import PartitionSpec as P

F32 = jnp.float32
BF16 = jnp.bfloat16
MESH = pl.DeviceIdType.MESH
VM = pl.BlockSpec(memory_space=pltpu.VMEM)
HBM = pl.BlockSpec(memory_space=pltpu.HBM)


def place():
    k = lax.axis_index("rows")
    j = lax.axis_index("chan")
    return k, j // 4, (j // 2) % 2, j % 2


def dev(k, yx, zh, c):
    return {"rows": k, "chan": (yx * 2 + zh) * 2 + c}


def plane_peer(a, i):
    other = (a + i) % 32
    return other // 2, other % 2


def far_first(i):
    return 8 + (i // 2) * (1 - 2 * (i % 2))


def z_dev(z, yx, c):
    z = z % 16
    return dev(z % 8, yx, z // 8, c)


def lay_out(order_ref, x_ref, g_ref, out_ref, ge, go, xs, c):
    pos = lax.broadcasted_iota(jnp.int32, (49, 128), 0)
    lane = lax.broadcasted_iota(jnp.int32, (49, 128), 1)
    slot = (pos // 7) * 8 + pos % 7
    low = jnp.where(lane == slot, 1.0, 0.0).astype(BF16)
    high = jnp.where(lane == slot + 64, 1.0, 0.0).astype(BF16)
    for u in range(16):
        ge[pl.ds(u * 8, 8), :] = g_ref[order_ref[0, 2 * u]].astype(F32)
        go[pl.ds(u * 8, 8), :] = g_ref[order_ref[0, 2 * u + 1]].astype(F32)
    grads = jnp.dot(ge[...].astype(BF16), low, preferred_element_type=F32) + jnp.dot(
        go[...].astype(BF16), high, preferred_element_type=F32
    )
    grads = grads.reshape(16, 8, 128)
    unit = lax.broadcasted_iota(jnp.int32, (16, 32), 0)
    example = lax.broadcasted_iota(jnp.int32, (16, 32), 1)
    even = jnp.zeros((16, 32), F32)
    odd = jnp.zeros((16, 32), F32)
    for u in range(16):
        even = jnp.where((unit == u) & (example == order_ref[0, 2 * u]), 1.0, even)
        odd = jnp.where((unit == u) & (example == order_ref[0, 2 * u + 1]), 1.0, odd)
    even = even.astype(BF16)
    odd = odd.astype(BF16)
    for ch in range(8):
        part = x_ref[:, ch, :]
        dims = (((0,), (0,)), ((), ()))
        at_low = lax.dot_general(part, low, dims, preferred_element_type=F32).astype(BF16)
        at_high = lax.dot_general(part, high, dims, preferred_element_type=F32).astype(BF16)
        xs[:, ch, :] = jnp.dot(even, at_low, preferred_element_type=F32) + jnp.dot(
            odd, at_high, preferred_element_type=F32
        )
    inputs = xs[...]
    first = jnp.where(c == 0, grads, inputs)
    second = jnp.where(c == 0, inputs, grads)
    out_ref[...] = jnp.concatenate([first, second], axis=1).astype(BF16)


def block(rows_ref, piv_ref, out_ref, ag, ax, bg, bx, gg, xx, yx):
    mask = lax.broadcasted_iota(jnp.int32, (16, 16, 128), 1) < 8
    for z2 in range(2):
        for u in range(4):
            even = rows_ref[pl.ds(z2 * 32, 16), u]
            odd = rows_ref[pl.ds(z2 * 32 + 16, 16), u]
            ag[pl.ds(z2 * 256, 256), pl.ds(u * 128, 128)] = jnp.where(mask, even, odd).reshape(256, 128)
            ax[pl.ds(z2 * 256, 256), pl.ds(u * 128, 128)] = jnp.where(mask, odd, even).reshape(256, 128)
            even = piv_ref[(u * 2 + z2) * 2]
            odd = piv_ref[(u * 2 + z2) * 2 + 1]
            bg[pl.ds(z2 * 256, 256), pl.ds(u * 128, 128)] = jnp.where(mask, even, odd).reshape(256, 128)
            bx[pl.ds(z2 * 256, 256), pl.ds(u * 128, 128)] = jnp.where(mask, odd, even).reshape(256, 128)
    dims = (((0,), (0,)), ((), ()))
    gg[...] = lax.dot_general(ag[...], bg[...], dims, preferred_element_type=F32)
    xx[...] = lax.dot_general(ax[...], bx[...], dims, preferred_element_type=F32)
    lanes = lax.broadcasted_iota(jnp.int32, (128, 128), 0)
    cols = lax.broadcasted_iota(jnp.int32, (128, 128), 1)
    piv0 = 16 * (yx % 2) + 2 * ((yx // 4) * 2 + (yx % 4) // 2)
    pieces = jnp.zeros((8, 128), F32)
    for t in range(4):
        col = pl.ds(t * 128, 128)
        summed = []
        for e in range(8):
            wide = xx[pl.ds(e * 64, 64), col]
            wide = (
                wide
                + pltpu.roll(pltpu.roll(wide, 1, 0), 1, 1)
                + pltpu.roll(pltpu.roll(wide, 63, 0), 127, 1)
            )
            wide = (
                wide
                + pltpu.roll(pltpu.roll(wide, 8, 0), 8, 1)
                + pltpu.roll(pltpu.roll(wide, 56, 0), 120, 1)
            )
            summed.append(jnp.sum(gg[pl.ds(e * 64, 64), col] * wide, axis=0, keepdims=True))
        folded = jnp.concatenate(summed, axis=0)
        spread = jnp.where(cols == piv0 + 32 * t + lanes // 64, 1.0, 0.0)
        pieces = pieces + jnp.dot(folded, spread, precision=lax.Precision.HIGHEST, preferred_element_type=F32)
    out_ref[...] = pieces


def eliminate(left, right, store):
    full = (8, 128)
    for m0 in range(16):
        j0 = 8 * m0
        rows = [jnp.broadcast_to(left[m0][i:i + 1, :], full) for i in range(8)]
        rights = [jnp.broadcast_to(right[m0][i:i + 1, :], full) for i in range(8)]
        cols = [jnp.broadcast_to(left[m0][:, j0 + l:j0 + l + 1], full) for l in range(8)]
        e = [[jnp.broadcast_to(cols[l][i:i + 1, :], full) if i <= l else None for l in range(8)] for i in range(8)]
        inverse, ratio = [], {}
        for i in range(8):
            inverse.append(1.0 / e[i][i])
            for l in range(i + 1, 8):
                ratio[i, l] = e[i][l] * inverse[i]
            for l in range(i + 1, 8):
                for n in range(l, 8):
                    e[l][n] = e[l][n] - ratio[i, l] * e[i][n]
                rows[l] = rows[l] - ratio[i, l] * rows[i]
                rights[l] = rights[l] - ratio[i, l] * rights[i]
        for i in range(8):
            store(j0 + i, rights[i] * lax.rsqrt(e[i][i]))
        if m0 == 15:
            break
        for i in reversed(range(8)):
            rows[i] = rows[i] * inverse[i]
            rights[i] = rights[i] * inverse[i]
            for l in range(i + 1, 8):
                rows[i] = rows[i] - ratio[i, l] * rows[l]
                rights[i] = rights[i] - ratio[i, l] * rights[l]
        for m in range(m0 + 1, 16):
            block = left[m]
            for i in range(8):
                factor = jnp.broadcast_to(block[:, j0 + i:j0 + i + 1], full)
                left[m] = left[m] - factor * rows[i]
                right[m] = right[m] - factor * rights[i]


def factor(panel_ref, ridge_ref, gram_ref, factor_ref, f_ref, k):
    gram_ref[pl.ds(0, 16), :] = panel_ref[k]
    gram_ref[pl.ds(16, 16), :] = panel_ref[8]
    gram = gram_ref[...]
    diag = panel_ref[0:8].reshape(128, 128)
    row = lax.broadcasted_iota(jnp.int32, (128, 128), 0)
    col = lax.broadcasted_iota(jnp.int32, (128, 128), 1)
    system = 0.5 * (diag + diag.T) + jnp.where(row == col, ridge_ref[...], 0.0)
    right = jnp.concatenate([gram, jnp.zeros((96, 128), F32)], axis=0).T
    left = [system[8 * m:8 * m + 8] for m in range(16)]
    right = [right[8 * m:8 * m + 8] for m in range(16)]

    def store(row, values):
        f_ref[pl.ds(row, 1), :] = values[0:1]

    eliminate(left, right, store)
    factor_ref[...] = f_ref[...].T[:32]


def panel_kernel(order_hbm, x_hbm, g_hbm, ridge_hbm, gram_ref, factor_ref,
                 out_ref, f_ref, ridge_ref, order_ref, x_ref, g_ref, ge, go, xs, t_ref, mate_ref, rows_ref, piv_ref, ag, ax, bg, bx, gg, xx, part_ref, parts, plane_rows,
                 mate_sem, row_send, row_recv, piv_send, piv_recv, hop_send, in_sem,
                 sib_send, sib_recv, send1, recv1, send2, recv2, recv3):
    k, yx, zh, c = place()
    z = zh * 8 + k
    a = yx * 2 + c
    away = (k + yx) % 2
    mate_dev = dev(k, yx, 1 - zh, c)
    sib_dev = dev(k, yx, zh, 1 - c)

    barrier = pltpu.get_barrier_semaphore()

    def signal(target):
        pl.semaphore_signal(barrier, inc=1, device_id=target, device_id_type=MESH)

    @pl.loop(1, 16)
    def _(i):
        signal(z_dev(z + far_first(i), yx, c))

    @pl.when(away == 1)
    def _():
        @pl.loop(0, 16)
        def _(i):
            signal(z_dev(z + 3, i, c))
            signal(z_dev(z + 13, i, c))

    operands = [
        pltpu.make_async_copy(src, dst, in_sem.at[n])
        for n, (src, dst) in enumerate(((order_hbm, order_ref), (x_hbm, x_ref), (g_hbm, g_ref), (ridge_hbm, ridge_ref)))
    ]
    for copy in operands:
        copy.start()

    @pl.loop(1, 32)
    def _(i):
        yx2, c2 = plane_peer(a, i)
        signal(dev(k, yx2, zh, c2))

    for copy in operands:
        copy.wait()
    lay_out(order_ref, x_ref, g_ref, t_ref, ge, go, xs, c)
    pl.semaphore_wait(barrier, 62)

    def remote(src, dst, send, recv, target):
        return pltpu.make_async_remote_copy(
            src_ref=src, dst_ref=dst, send_sem=send, recv_sem=recv, device_id=target, device_id_type=MESH)

    def drain(ref, sem):
        pltpu.make_async_copy(ref, ref, sem).wait()

    to_mate = remote(t_ref.at[pl.ds(8 * (1 - zh), 8)], mate_ref, mate_sem.at[0], mate_sem.at[1], mate_dev)
    to_mate.start()

    def chunk_of(src_z):
        src_z = (src_z + 32) % 16
        return (((src_z % 8) // 2) * 2 + src_z // 8) * 2 + c

    own_chunk = chunk_of(z)
    for step in (3, 13, 0):
        for u in range(8):
            target = (u // 2) * 4 + 2 * (u % 2) + k % 2
            recv = piv_recv.at[{3: 3, 13: 13, 0: 0}[step]]
            tile = remote(t_ref.at[u], piv_ref.at[own_chunk, yx], piv_send.at[0], recv, z_dev(z + step, target, c))
            if step:
                tile.start()
                continue

            @pl.when(target == yx)
            def _():
                pltpu.make_async_copy(t_ref.at[u], piv_ref.at[own_chunk, yx], recv).start()

            @pl.when(target != yx)
            def _():
                tile.start()

    def send_rows(src_ref, base, slot):
        @pl.loop(1, 32)
        def _(i):
            yx2, c2 = plane_peer(a, i)
            remote(src_ref.at[pl.ds(base + 4 * c2, 4)], rows_ref.at[slot], row_send.at[0], row_recv.at[0],
                   dev(k, yx2, zh, c2)).start()

        pltpu.make_async_copy(src_ref.at[pl.ds(base + 4 * c, 4)], rows_ref.at[slot], row_recv.at[0]).start()

    def piv_copy(chunk, target, send, recv):
        return remote(piv_ref.at[chunk], piv_ref.at[chunk], send, recv, target)

    def sib_copy(chunk):
        return piv_copy(chunk, sib_dev, sib_send.at[0], sib_recv.at[0])

    def hop(off, step):
        return piv_copy(chunk_of(z - off), z_dev(z + 16 + step, yx, c), hop_send.at[0], piv_recv.at[(off + step) % 16])

    def arrived(off, steps=()):
        drain(piv_ref.at[chunk_of(z - off)], piv_recv.at[off % 16])
        for step in steps:
            hop(off, step).start()
        sib_copy(chunk_of(z - off)).start()

    send_rows(t_ref, 8 * zh, (zh * 2 + c) * 16 + yx)

    @pl.when(away == 0)
    def _():
        arrived(0, (1, -1))

    @pl.when(away == 1)
    def _():
        arrived(3, (3, 1, -1))
        arrived(-3, (-3, -1, 1))

    to_mate.wait_recv()
    send_rows(mate_ref, 0, ((1 - zh) * 2 + c) * 16 + yx)

    @pl.when(away == 0)
    def _():
        arrived(6, (2, 1, -1))
        arrived(-6, (-1, 1))
        for off in (2, -2, 4, -4, 8):
            arrived(off)

    @pl.when(away == 1)
    def _():
        for off in (1, -1, 5, -5, 7, -7):
            arrived(off)

    to_mate.wait_send()

    @pl.when(away == 0)
    def _():
        drain(rows_ref.at[pl.ds(0, 5)], piv_send.at[0])
        drain(rows_ref.at[pl.ds(0, 3), pl.ds(0, 1)], piv_send.at[0])
        drain(piv_ref.at[pl.ds(0, 7)], hop_send.at[0])

    @pl.when(away == 1)
    def _():
        drain(rows_ref.at[pl.ds(0, 6)], piv_send.at[0])
        drain(piv_ref.at[pl.ds(0, 6)], hop_send.at[0])

    drain(rows_ref.at[pl.ds(0, 62)], row_send.at[0])
    drain(piv_ref.at[pl.ds(0, 8)], sib_send.at[0])
    drain(rows_ref, row_recv.at[0])
    drain(piv_ref.at[pl.ds(0, 8)], sib_recv.at[0])

    block(rows_ref, piv_ref, part_ref, ag, ax, bg, bx, gg, xx, yx)

    slot = c * 16 + yx

    @pl.loop(1, 32)
    def _(i):
        yx2, c2 = plane_peer(a, i)
        remote(part_ref, parts.at[slot], send1.at[0], recv1.at[0], dev(k, yx2, zh, c2)).start()

    pltpu.make_async_copy(part_ref, parts.at[slot], recv1.at[0]).start()
    drain(parts, recv1.at[0])
    for c2 in range(2):
        plane_rows[pl.ds(c2 * 8, 8), :] = jnp.sum(parts[pl.ds(c2 * 16, 16)], axis=0)

    @pl.when(zh == 0)
    def _():
        @pl.loop(1, 16)
        def _(i):
            remote(plane_rows, out_ref.at[k], send2.at[0], recv2.at[0], z_dev(z + far_first(i), yx, c)).start()

        pltpu.make_async_copy(plane_rows, out_ref.at[k], recv2.at[0]).start()

    @pl.when(zh == 1)
    def _():
        remote(plane_rows, out_ref.at[8], send2.at[0], recv3.at[0], mate_dev).start()
        pltpu.make_async_copy(plane_rows, out_ref.at[8], recv3.at[0]).start()

    drain(out_ref.at[pl.ds(0, 8)], recv2.at[0])
    drain(out_ref.at[8], recv3.at[0])
    factor(out_ref, ridge_ref, gram_ref, factor_ref, f_ref, k)
    drain(parts.at[pl.ds(0, 31)], send1.at[0])

    @pl.when(zh == 0)
    def _():
        drain(parts.at[pl.ds(0, 30)], send2.at[0])

    @pl.when(zh == 1)
    def _():
        drain(plane_rows, send2.at[0])


def panel(order, x, g, ridge):
    out = jax.ShapeDtypeStruct((32, 128), F32)
    dma = pltpu.SemaphoreType.DMA
    return pl.pallas_call(
        panel_kernel,
        out_shape=[out, out],
        in_specs=[HBM] * 4,
        out_specs=[VM, VM],
        scratch_shapes=[
            pltpu.VMEM((9, 16, 128), F32),
            pltpu.VMEM((128, 128), F32),
            pltpu.VMEM((1, 128), F32),
            pltpu.SMEM((1, 32), jnp.int32),
            pltpu.VMEM((49, 8, 32), BF16),
            pltpu.VMEM((32, 8, 49), BF16),
            pltpu.VMEM((128, 49), F32),
            pltpu.VMEM((128, 49), F32),
            pltpu.VMEM((16, 8, 128), F32),
            pltpu.VMEM((16, 16, 128), BF16),
            pltpu.VMEM((8, 16, 128), BF16),
            pltpu.VMEM((64, 4, 16, 128), BF16),
            pltpu.VMEM((16, 16, 16, 128), BF16),
        ]
        + [pltpu.VMEM((512, 512), BF16)] * 4
        + [pltpu.VMEM((512, 512), F32)] * 2
        + [pltpu.VMEM((8, 128), F32), pltpu.VMEM((32, 8, 128), F32), pltpu.VMEM((16, 128), F32)]
        + [dma((n,)) for n in (2, 1, 1, 1, 16, 1, 4, 1, 1, 1, 1, 1, 1, 1)],
        compiler_params=pltpu.CompilerParams(
            collective_id=0, has_side_effects=True, vmem_limit_bytes=56 * 1024 * 1024),
        name="panel",
    )(order, x, g, ridge)


def local(activations, cotangents, ordering, ridge):
    x = activations.transpose(1, 2, 3, 0).reshape(49, 8, 32)
    return tuple(panel(ordering, x, cotangents, ridge.reshape(1, 128)))


def solution(mesh):
    return jax.shard_map(
        local,
        mesh=mesh,
        in_specs=(P("rows", None, None, "chan"), P("rows", "chan", None), P("rows", None), P()),
        out_specs=(P("rows", None), P("rows", None)),
        check_vma=False,
    )
```

```python
import jax
import jax.numpy as jnp
from jax import lax
from jax.experimental import pallas as pl
from jax.experimental.pallas import tpu as pltpu
from jax.sharding import PartitionSpec as P

F32 = jnp.float32
BF16 = jnp.bfloat16
MESH = pl.DeviceIdType.MESH
VM = pl.BlockSpec(memory_space=pltpu.VMEM)
HBM = pl.BlockSpec(memory_space=pltpu.HBM)


def place():
    k = lax.axis_index("rows")
    j = lax.axis_index("chan")
    return k, j // 4, (j // 2) % 2, j % 2


def dev(k, yx, zh, c):
    return {"rows": k, "chan": (yx * 2 + zh) * 2 + c}


def plane_peers(yx, c):
    steps = sorted(((dy, dx) for dy in range(4) for dx in range(4)),
                   key=lambda step: -sum(min(d, 4 - d) for d in step))
    for dy, dx in steps:
        for flip in (0, 1):
            if dy or dx or flip:
                yield ((yx // 4 + dy) % 4) * 4 + (yx + dx) % 4, (c + flip) % 2


def far_first(i):
    return 8 + (i // 2) * (1 - 2 * (i % 2))


def z_dev(z, yx, c):
    z = z % 16
    return dev(z % 8, yx, z // 8, c)


def lay_out(order_ref, x_ref, g_ref, out_ref, ge, go, xs, c):
    pos = lax.broadcasted_iota(jnp.int32, (49, 128), 0)
    lane = lax.broadcasted_iota(jnp.int32, (49, 128), 1)
    slot = (pos // 7) * 8 + pos % 7
    low = jnp.where(lane == slot, 1.0, 0.0).astype(BF16)
    high = jnp.where(lane == slot + 64, 1.0, 0.0).astype(BF16)
    for u in range(16):
        ge[pl.ds(u * 8, 8), :] = g_ref[order_ref[0, 2 * u]].astype(F32)
        go[pl.ds(u * 8, 8), :] = g_ref[order_ref[0, 2 * u + 1]].astype(F32)
    grads = jnp.dot(ge[...].astype(BF16), low, preferred_element_type=F32) + jnp.dot(
        go[...].astype(BF16), high, preferred_element_type=F32
    )
    grads = grads.reshape(16, 8, 128)
    unit = lax.broadcasted_iota(jnp.int32, (16, 32), 0)
    example = lax.broadcasted_iota(jnp.int32, (16, 32), 1)
    even = jnp.zeros((16, 32), F32)
    odd = jnp.zeros((16, 32), F32)
    for u in range(16):
        even = jnp.where((unit == u) & (example == order_ref[0, 2 * u]), 1.0, even)
        odd = jnp.where((unit == u) & (example == order_ref[0, 2 * u + 1]), 1.0, odd)
    even = even.astype(BF16)
    odd = odd.astype(BF16)
    for ch in range(8):
        part = x_ref[:, ch, :]
        dims = (((0,), (0,)), ((), ()))
        at_low = lax.dot_general(part, low, dims, preferred_element_type=F32).astype(BF16)
        at_high = lax.dot_general(part, high, dims, preferred_element_type=F32).astype(BF16)
        xs[:, ch, :] = jnp.dot(even, at_low, preferred_element_type=F32) + jnp.dot(
            odd, at_high, preferred_element_type=F32
        )
    inputs = xs[...]
    first = jnp.where(c == 0, grads, inputs)
    second = jnp.where(c == 0, inputs, grads)
    out_ref[...] = jnp.concatenate([first, second], axis=1).astype(BF16)


def block(rows_ref, piv_ref, out_ref, ag, ax, bg, bx, gg, xx, yx):
    mask = lax.broadcasted_iota(jnp.int32, (16, 16, 128), 1) < 8
    for z2 in range(2):
        for u in range(4):
            even = rows_ref[pl.ds(z2 * 32, 16), u]
            odd = rows_ref[pl.ds(z2 * 32 + 16, 16), u]
            ag[pl.ds(z2 * 256, 256), pl.ds(u * 128, 128)] = jnp.where(mask, even, odd).reshape(256, 128)
            ax[pl.ds(z2 * 256, 256), pl.ds(u * 128, 128)] = jnp.where(mask, odd, even).reshape(256, 128)
            even = piv_ref[(u * 2 + z2) * 2]
            odd = piv_ref[(u * 2 + z2) * 2 + 1]
            bg[pl.ds(z2 * 256, 256), pl.ds(u * 128, 128)] = jnp.where(mask, even, odd).reshape(256, 128)
            bx[pl.ds(z2 * 256, 256), pl.ds(u * 128, 128)] = jnp.where(mask, odd, even).reshape(256, 128)
    dims = (((0,), (0,)), ((), ()))
    gg[...] = lax.dot_general(ag[...], bg[...], dims, preferred_element_type=F32)
    xx[...] = lax.dot_general(ax[...], bx[...], dims, preferred_element_type=F32)
    lanes = lax.broadcasted_iota(jnp.int32, (128, 128), 0)
    cols = lax.broadcasted_iota(jnp.int32, (128, 128), 1)
    piv0 = 16 * (yx % 2) + 2 * ((yx // 4) * 2 + (yx % 4) // 2)
    pieces = jnp.zeros((8, 128), F32)
    for t in range(4):
        col = pl.ds(t * 128, 128)
        summed = []
        for e in range(8):
            wide = xx[pl.ds(e * 64, 64), col]
            wide = (
                wide
                + pltpu.roll(pltpu.roll(wide, 1, 0), 1, 1)
                + pltpu.roll(pltpu.roll(wide, 63, 0), 127, 1)
            )
            wide = (
                wide
                + pltpu.roll(pltpu.roll(wide, 8, 0), 8, 1)
                + pltpu.roll(pltpu.roll(wide, 56, 0), 120, 1)
            )
            summed.append(jnp.sum(gg[pl.ds(e * 64, 64), col] * wide, axis=0, keepdims=True))
        folded = jnp.concatenate(summed, axis=0)
        spread = jnp.where(cols == piv0 + 32 * t + lanes // 64, 1.0, 0.0)
        pieces = pieces + jnp.dot(folded, spread, precision=lax.Precision.HIGHEST, preferred_element_type=F32)
    out_ref[...] = pieces


def eliminate(left, right, store):
    full = (8, 128)
    for m0 in range(16):
        j0 = 8 * m0
        rows = [jnp.broadcast_to(left[m0][i:i + 1, :], full) for i in range(8)]
        rights = [jnp.broadcast_to(right[m0][i:i + 1, :], full) for i in range(8)]
        cols = [jnp.broadcast_to(left[m0][:, j0 + l:j0 + l + 1], full) for l in range(8)]
        e = [[jnp.broadcast_to(cols[l][i:i + 1, :], full) if i <= l else None for l in range(8)] for i in range(8)]
        inverse, ratio = [], {}
        for i in range(8):
            inverse.append(1.0 / e[i][i])
            for l in range(i + 1, 8):
                ratio[i, l] = e[i][l] * inverse[i]
            for l in range(i + 1, 8):
                for n in range(l, 8):
                    e[l][n] = e[l][n] - ratio[i, l] * e[i][n]
                rows[l] = rows[l] - ratio[i, l] * rows[i]
                rights[l] = rights[l] - ratio[i, l] * rights[i]
        for i in range(8):
            store(j0 + i, rights[i] * lax.rsqrt(e[i][i]))
        if m0 == 15:
            break
        for i in reversed(range(8)):
            rows[i] = rows[i] * inverse[i]
            rights[i] = rights[i] * inverse[i]
            for l in range(i + 1, 8):
                rows[i] = rows[i] - ratio[i, l] * rows[l]
                rights[i] = rights[i] - ratio[i, l] * rights[l]
        for m in range(m0 + 1, 16):
            block = left[m]
            for i in range(8):
                factor = jnp.broadcast_to(block[:, j0 + i:j0 + i + 1], full)
                left[m] = left[m] - factor * rows[i]
                right[m] = right[m] - factor * rights[i]


def factor(panel_ref, ridge_ref, gram_ref, factor_ref, f_ref, k):
    gram_ref[pl.ds(0, 16), :] = panel_ref[k]
    gram_ref[pl.ds(16, 16), :] = panel_ref[8]
    gram = gram_ref[...]
    diag = panel_ref[0:8].reshape(128, 128)
    row = lax.broadcasted_iota(jnp.int32, (128, 128), 0)
    col = lax.broadcasted_iota(jnp.int32, (128, 128), 1)
    system = 0.5 * (diag + diag.T) + jnp.where(row == col, ridge_ref[...], 0.0)
    right = jnp.concatenate([gram, jnp.zeros((96, 128), F32)], axis=0).T
    left = [system[8 * m:8 * m + 8] for m in range(16)]
    right = [right[8 * m:8 * m + 8] for m in range(16)]

    def store(row, values):
        f_ref[pl.ds(row, 1), :] = values[0:1]

    eliminate(left, right, store)
    factor_ref[...] = f_ref[...].T[:32]


def panel_kernel(order_hbm, x_hbm, g_hbm, ridge_hbm, both_ref,
                 out_ref, f_ref, ridge_ref, order_ref, x_ref, g_ref, ge, go, xs, t_ref, mate_ref, rows_ref, piv_ref, ag, ax, bg, bx, gg, xx, part_ref, parts, plane_rows,
                 mate_sem, row_send, row_recv, piv_send, piv_recv, hop_send, in_sem,
                 sib_send, sib_recv, send1, recv1, send2, recv2, recv3):
    k, yx, zh, c = place()
    z = zh * 8 + k
    away = (k + yx) % 2
    mate_dev = dev(k, yx, 1 - zh, c)
    sib_dev = dev(k, yx, zh, 1 - c)

    barrier = pltpu.get_barrier_semaphore()

    def signal(target):
        pl.semaphore_signal(barrier, inc=1, device_id=target, device_id_type=MESH)

    @pl.loop(1, 16)
    def _(i):
        signal(z_dev(z + far_first(i), yx, c))

    @pl.when(away == 1)
    def _():
        @pl.loop(0, 16)
        def _(i):
            signal(z_dev(z + 3, i, c))
            signal(z_dev(z + 13, i, c))

    operands = [
        pltpu.make_async_copy(src, dst, in_sem.at[n])
        for n, (src, dst) in enumerate(((order_hbm, order_ref), (x_hbm, x_ref), (g_hbm, g_ref), (ridge_hbm, ridge_ref)))
    ]
    for copy in operands:
        copy.start()

    for yx2, c2 in plane_peers(yx, c):
        signal(dev(k, yx2, zh, c2))

    for copy in operands:
        copy.wait()
    lay_out(order_ref, x_ref, g_ref, t_ref, ge, go, xs, c)
    pl.semaphore_wait(barrier, 62)

    def remote(src, dst, send, recv, target):
        return pltpu.make_async_remote_copy(
            src_ref=src, dst_ref=dst, send_sem=send, recv_sem=recv, device_id=target, device_id_type=MESH)

    def drain(ref, sem):
        pltpu.make_async_copy(ref, ref, sem).wait()

    to_mate = remote(t_ref.at[pl.ds(8 * (1 - zh), 8)], mate_ref, mate_sem.at[0], mate_sem.at[1], mate_dev)

    def chunk_of(src_z):
        src_z = (src_z + 32) % 16
        return (((src_z % 8) // 2) * 2 + src_z // 8) * 2 + c

    own_chunk = chunk_of(z)
    for step in (3, 13, 0):
        for u in range(8):
            target = (u // 2) * 4 + 2 * (u % 2) + k % 2
            recv = piv_recv.at[{3: 3, 13: 13, 0: 0}[step]]
            tile = remote(t_ref.at[u], piv_ref.at[own_chunk, yx], piv_send.at[0], recv, z_dev(z + step, target, c))
            if step:
                tile.start()
                continue

            @pl.when(target == yx)
            def _():
                pltpu.make_async_copy(t_ref.at[u], piv_ref.at[own_chunk, yx], recv).start()

            @pl.when(target != yx)
            def _():
                tile.start()

    def send_rows(src_ref, base, slot):
        for yx2, c2 in plane_peers(yx, c):
            remote(src_ref.at[pl.ds(base + 4 * c2, 4)], rows_ref.at[slot], row_send.at[0], row_recv.at[0],
                   dev(k, yx2, zh, c2)).start()

        pltpu.make_async_copy(src_ref.at[pl.ds(base + 4 * c, 4)], rows_ref.at[slot], row_recv.at[0]).start()

    def piv_copy(chunk, target, send, recv):
        return remote(piv_ref.at[chunk], piv_ref.at[chunk], send, recv, target)

    def sib_copy(chunk):
        return piv_copy(chunk, sib_dev, sib_send.at[0], sib_recv.at[0])

    def hop(off, step):
        return piv_copy(chunk_of(z - off), z_dev(z + 16 + step, yx, c), hop_send.at[0], piv_recv.at[(off + step) % 16])

    def arrived(off, steps=()):
        drain(piv_ref.at[chunk_of(z - off)], piv_recv.at[off % 16])
        for step in steps:
            hop(off, step).start()
        sib_copy(chunk_of(z - off)).start()

    to_mate.start()
    send_rows(t_ref, 8 * zh, (zh * 2 + c) * 16 + yx)

    @pl.when(away == 0)
    def _():
        arrived(0, (1, -1))

    @pl.when(away == 1)
    def _():
        arrived(3, (3, 1, -1))
        arrived(-3, (-3, -1, 1))

    to_mate.wait_recv()
    send_rows(mate_ref, 0, ((1 - zh) * 2 + c) * 16 + yx)

    @pl.when(away == 0)
    def _():
        arrived(6, (2, 1, -1))
        arrived(-6, (-1, 1))
        for off in (2, -2, 4, -4, 8):
            arrived(off)

    @pl.when(away == 1)
    def _():
        for off in (1, -1, 5, -5, 7, -7):
            arrived(off)

    to_mate.wait_send()

    @pl.when(away == 0)
    def _():
        drain(rows_ref.at[pl.ds(0, 5)], piv_send.at[0])
        drain(rows_ref.at[pl.ds(0, 3), pl.ds(0, 1)], piv_send.at[0])
        drain(piv_ref.at[pl.ds(0, 7)], hop_send.at[0])

    @pl.when(away == 1)
    def _():
        drain(rows_ref.at[pl.ds(0, 6)], piv_send.at[0])
        drain(piv_ref.at[pl.ds(0, 6)], hop_send.at[0])

    drain(rows_ref.at[pl.ds(0, 62)], row_send.at[0])
    drain(piv_ref.at[pl.ds(0, 8)], sib_send.at[0])
    drain(rows_ref, row_recv.at[0])
    drain(piv_ref.at[pl.ds(0, 8)], sib_recv.at[0])

    block(rows_ref, piv_ref, part_ref, ag, ax, bg, bx, gg, xx, yx)

    slot = c * 16 + yx

    for yx2, c2 in plane_peers(yx, c):
        remote(part_ref, parts.at[slot], send1.at[0], recv1.at[0], dev(k, yx2, zh, c2)).start()

    pltpu.make_async_copy(part_ref, parts.at[slot], recv1.at[0]).start()
    drain(parts, recv1.at[0])
    for c2 in range(2):
        plane_rows[pl.ds(c2 * 8, 8), :] = jnp.sum(parts[pl.ds(c2 * 16, 16)], axis=0)

    @pl.when(zh == 0)
    def _():
        @pl.loop(1, 16)
        def _(i):
            remote(plane_rows, out_ref.at[k], send2.at[0], recv2.at[0], z_dev(z + far_first(i), yx, c)).start()

        pltpu.make_async_copy(plane_rows, out_ref.at[k], recv2.at[0]).start()

    @pl.when(zh == 1)
    def _():
        remote(plane_rows, out_ref.at[8], send2.at[0], recv3.at[0], mate_dev).start()
        pltpu.make_async_copy(plane_rows, out_ref.at[8], recv3.at[0]).start()

    drain(out_ref.at[pl.ds(0, 8)], recv2.at[0])
    drain(out_ref.at[8], recv3.at[0])
    factor(out_ref, ridge_ref, both_ref.at[0], both_ref.at[1], f_ref, k)
    drain(parts.at[pl.ds(0, 31)], send1.at[0])

    @pl.when(zh == 0)
    def _():
        drain(parts.at[pl.ds(0, 30)], send2.at[0])

    @pl.when(zh == 1)
    def _():
        drain(plane_rows, send2.at[0])


def panel(order, x, g, ridge):
    dma = pltpu.SemaphoreType.DMA
    return pl.pallas_call(
        panel_kernel,
        out_shape=jax.ShapeDtypeStruct((2, 32, 128), F32),
        in_specs=[HBM] * 4,
        out_specs=VM,
        scratch_shapes=[
            pltpu.VMEM((9, 16, 128), F32),
            pltpu.VMEM((128, 128), F32),
            pltpu.VMEM((1, 128), F32),
            pltpu.SMEM((1, 32), jnp.int32),
            pltpu.VMEM((49, 8, 32), BF16),
            pltpu.VMEM((32, 8, 49), BF16),
            pltpu.VMEM((128, 49), F32),
            pltpu.VMEM((128, 49), F32),
            pltpu.VMEM((16, 8, 128), F32),
            pltpu.VMEM((16, 16, 128), BF16),
            pltpu.VMEM((8, 16, 128), BF16),
            pltpu.VMEM((64, 4, 16, 128), BF16),
            pltpu.VMEM((16, 16, 16, 128), BF16),
        ]
        + [pltpu.VMEM((512, 512), BF16)] * 4
        + [pltpu.VMEM((512, 512), F32)] * 2
        + [pltpu.VMEM((8, 128), F32), pltpu.VMEM((32, 8, 128), F32), pltpu.VMEM((16, 128), F32)]
        + [dma((n,)) for n in (2, 1, 1, 1, 16, 1, 4, 1, 1, 1, 1, 1, 1, 1)],
        compiler_params=pltpu.CompilerParams(
            collective_id=0, has_side_effects=True, vmem_limit_bytes=56 * 1024 * 1024),
        name="panel",
    )(order, x, g, ridge)


def local(activations, cotangents, ordering, ridge):
    x = activations.transpose(1, 2, 3, 0).reshape(49, 8, 32)
    both = panel(ordering, x, cotangents, ridge.reshape(1, 128))
    return both[0], both[1]


def solution(mesh):
    return jax.shard_map(
        local,
        mesh=mesh,
        in_specs=(P("rows", None, None, "chan"), P("rows", "chan", None), P("rows", None), P()),
        out_specs=(P("rows", None), P("rows", None)),
        check_vma=False,
    )
```

```python
import jax
import jax.numpy as jnp
from jax import lax
from jax.experimental import pallas as pl
from jax.experimental.pallas import tpu as pltpu
from jax.sharding import PartitionSpec as P

F32 = jnp.float32
BF16 = jnp.bfloat16
MESH = pl.DeviceIdType.MESH
VM = pl.BlockSpec(memory_space=pltpu.VMEM)
HBM = pl.BlockSpec(memory_space=pltpu.HBM)


def place():
    k = lax.axis_index("rows")
    j = lax.axis_index("chan")
    return k, j // 4, (j // 2) % 2, j % 2


def dev(k, yx, zh, c):
    return {"rows": k, "chan": (yx * 2 + zh) * 2 + c}


def plane_peers(yx, c):
    steps = sorted(((dy, dx) for dy in range(4) for dx in range(4)),
                   key=lambda step: -sum(min(d, 4 - d) for d in step))
    for dy, dx in steps:
        for flip in (0, 1):
            if dy or dx or flip:
                yield ((yx // 4 + dy) % 4) * 4 + (yx + dx) % 4, (c + flip) % 2


def far_first(i):
    return 8 + (i // 2) * (1 - 2 * (i % 2))


def z_dev(z, yx, c):
    z = z % 16
    return dev(z % 8, yx, z // 8, c)


def lay_out(order_ref, x_ref, g_ref, out_ref, ge, go, xs, c):
    pos = lax.broadcasted_iota(jnp.int32, (49, 128), 0)
    lane = lax.broadcasted_iota(jnp.int32, (49, 128), 1)
    slot = (pos // 7) * 8 + pos % 7
    low = jnp.where(lane == slot, 1.0, 0.0).astype(BF16)
    high = jnp.where(lane == slot + 64, 1.0, 0.0).astype(BF16)
    for u in range(16):
        ge[pl.ds(u * 8, 8), :] = g_ref[order_ref[0, 2 * u]].astype(F32)
        go[pl.ds(u * 8, 8), :] = g_ref[order_ref[0, 2 * u + 1]].astype(F32)
    grads = jnp.dot(ge[...].astype(BF16), low, preferred_element_type=F32) + jnp.dot(
        go[...].astype(BF16), high, preferred_element_type=F32
    )
    grads = grads.reshape(16, 8, 128)
    unit = lax.broadcasted_iota(jnp.int32, (16, 32), 0)
    example = lax.broadcasted_iota(jnp.int32, (16, 32), 1)
    even = jnp.zeros((16, 32), F32)
    odd = jnp.zeros((16, 32), F32)
    for u in range(16):
        even = jnp.where((unit == u) & (example == order_ref[0, 2 * u]), 1.0, even)
        odd = jnp.where((unit == u) & (example == order_ref[0, 2 * u + 1]), 1.0, odd)
    even = even.astype(BF16)
    odd = odd.astype(BF16)
    for ch in range(8):
        part = x_ref[:, ch, :]
        dims = (((0,), (0,)), ((), ()))
        at_low = lax.dot_general(part, low, dims, preferred_element_type=F32).astype(BF16)
        at_high = lax.dot_general(part, high, dims, preferred_element_type=F32).astype(BF16)
        xs[:, ch, :] = jnp.dot(even, at_low, preferred_element_type=F32) + jnp.dot(
            odd, at_high, preferred_element_type=F32
        )
    inputs = xs[...]
    first = jnp.where(c == 0, grads, inputs)
    second = jnp.where(c == 0, inputs, grads)
    out_ref[...] = jnp.concatenate([first, second], axis=1).astype(BF16)


def split(z2, u, even, odd, grads, inputs):
    mask = lax.broadcasted_iota(jnp.int32, (16, 16, 128), 1) < 8
    at = pl.ds(z2 * 256, 256), pl.ds(u * 128, 128)
    grads[at] = jnp.where(mask, even, odd).reshape(256, 128)
    inputs[at] = jnp.where(mask, odd, even).reshape(256, 128)


def split_rows(rows_ref, ag, ax):
    for z2 in range(2):
        for u in range(4):
            split(z2, u, rows_ref[pl.ds(z2 * 32, 16), u], rows_ref[pl.ds(z2 * 32 + 16, 16), u], ag, ax)


def block(piv_ref, out_ref, ag, ax, bg, bx, gg, xx, yx):
    for z2 in range(2):
        for u in range(4):
            chunk = (u * 2 + z2) * 2
            split(z2, u, piv_ref[chunk], piv_ref[chunk + 1], bg, bx)
    dims = (((0,), (0,)), ((), ()))
    gg[...] = lax.dot_general(ag[...], bg[...], dims, preferred_element_type=F32)
    xx[...] = lax.dot_general(ax[...], bx[...], dims, preferred_element_type=F32)
    lanes = lax.broadcasted_iota(jnp.int32, (128, 128), 0)
    cols = lax.broadcasted_iota(jnp.int32, (128, 128), 1)
    piv0 = 16 * (yx % 2) + 2 * ((yx // 4) * 2 + (yx % 4) // 2)
    pieces = jnp.zeros((8, 128), F32)
    for t in range(4):
        col = pl.ds(t * 128, 128)
        summed = []
        for e in range(8):
            wide = xx[pl.ds(e * 64, 64), col]
            wide = (
                wide
                + pltpu.roll(pltpu.roll(wide, 1, 0), 1, 1)
                + pltpu.roll(pltpu.roll(wide, 63, 0), 127, 1)
            )
            wide = (
                wide
                + pltpu.roll(pltpu.roll(wide, 8, 0), 8, 1)
                + pltpu.roll(pltpu.roll(wide, 56, 0), 120, 1)
            )
            summed.append(jnp.sum(gg[pl.ds(e * 64, 64), col] * wide, axis=0, keepdims=True))
        folded = jnp.concatenate(summed, axis=0)
        spread = jnp.where(cols == piv0 + 32 * t + lanes // 64, 1.0, 0.0)
        pieces = pieces + jnp.dot(folded, spread, precision=lax.Precision.HIGHEST, preferred_element_type=F32)
    out_ref[...] = pieces


def eliminate(left, right, store):
    full = (8, 128)
    for m0 in range(16):
        j0 = 8 * m0
        rows = [jnp.broadcast_to(left[m0][i:i + 1, :], full) for i in range(8)]
        rights = [jnp.broadcast_to(right[m0][i:i + 1, :], full) for i in range(8)]
        cols = [jnp.broadcast_to(left[m0][:, j0 + l:j0 + l + 1], full) for l in range(8)]
        e = [[jnp.broadcast_to(cols[l][i:i + 1, :], full) if i <= l else None for l in range(8)] for i in range(8)]
        inverse, ratio = [], {}
        for i in range(8):
            inverse.append(1.0 / e[i][i])
            for l in range(i + 1, 8):
                ratio[i, l] = e[i][l] * inverse[i]
            for l in range(i + 1, 8):
                for n in range(l, 8):
                    e[l][n] = e[l][n] - ratio[i, l] * e[i][n]
                rows[l] = rows[l] - ratio[i, l] * rows[i]
                rights[l] = rights[l] - ratio[i, l] * rights[i]
        for i in range(8):
            store(j0 + i, rights[i] * lax.rsqrt(e[i][i]))
        if m0 == 15:
            break
        for i in reversed(range(8)):
            rows[i] = rows[i] * inverse[i]
            rights[i] = rights[i] * inverse[i]
            for l in range(i + 1, 8):
                rows[i] = rows[i] - ratio[i, l] * rows[l]
                rights[i] = rights[i] - ratio[i, l] * rights[l]
        for m in range(m0 + 1, 16):
            factors = [jnp.broadcast_to(left[m][:, j0 + i:j0 + i + 1], full) for i in range(8)]
            for side, vectors in ((left, rows), (right, rights)):
                terms = [f * v for f, v in zip(factors, vectors)]
                while len(terms) > 1:
                    terms = [terms[n] + terms[n + 1] for n in range(0, len(terms), 2)]
                side[m] = side[m] - terms[0]


def factor(panel_ref, ridge_ref, gram_ref, factor_ref, f_ref, k):
    gram_ref[pl.ds(0, 16), :] = panel_ref[k]
    gram_ref[pl.ds(16, 16), :] = panel_ref[8]
    gram = gram_ref[...]
    diag = panel_ref[0:8].reshape(128, 128)
    row = lax.broadcasted_iota(jnp.int32, (128, 128), 0)
    col = lax.broadcasted_iota(jnp.int32, (128, 128), 1)
    system = 0.5 * (diag + diag.T) + jnp.where(row == col, ridge_ref[...], 0.0)
    right = jnp.concatenate([gram, jnp.zeros((96, 128), F32)], axis=0).T
    left = [system[8 * m:8 * m + 8] for m in range(16)]
    right = [right[8 * m:8 * m + 8] for m in range(16)]

    def store(row, values):
        f_ref[pl.ds(row, 1), :] = values[0:1]

    eliminate(left, right, store)
    factor_ref[...] = f_ref[...].T[:32]


def panel_kernel(order_hbm, x_hbm, g_hbm, ridge_hbm, both_ref,
                 out_ref, f_ref, ridge_ref, order_ref, x_ref, g_ref, ge, go, xs, t_ref, mate_ref, rows_ref, piv_ref, ag, ax, bg, bx, gg, xx, part_ref, parts, plane_rows,
                 mate_sem, row_send, row_recv, piv_send, piv_recv, hop_send, in_sem,
                 sib_send, sib_recv, send1, recv1, send2, recv2, recv3):
    k, yx, zh, c = place()
    z = zh * 8 + k
    away = (k + yx) % 2
    mate_dev = dev(k, yx, 1 - zh, c)
    sib_dev = dev(k, yx, zh, 1 - c)

    barrier = pltpu.get_barrier_semaphore()

    def signal(target):
        pl.semaphore_signal(barrier, inc=1, device_id=target, device_id_type=MESH)

    @pl.loop(1, 16)
    def _(i):
        signal(z_dev(z + far_first(i), yx, c))

    @pl.when(away == 1)
    def _():
        @pl.loop(0, 16)
        def _(i):
            signal(z_dev(z + 3, i, c))
            signal(z_dev(z + 13, i, c))

    operands = [
        pltpu.make_async_copy(src, dst, in_sem.at[n])
        for n, (src, dst) in enumerate(((order_hbm, order_ref), (x_hbm, x_ref), (g_hbm, g_ref), (ridge_hbm, ridge_ref)))
    ]
    for copy in operands:
        copy.start()

    for yx2, c2 in plane_peers(yx, c):
        signal(dev(k, yx2, zh, c2))

    for copy in operands:
        copy.wait()
    lay_out(order_ref, x_ref, g_ref, t_ref, ge, go, xs, c)
    pl.semaphore_wait(barrier, 62)

    def remote(src, dst, send, recv, target):
        return pltpu.make_async_remote_copy(
            src_ref=src, dst_ref=dst, send_sem=send, recv_sem=recv, device_id=target, device_id_type=MESH)

    def drain(ref, sem):
        pltpu.make_async_copy(ref, ref, sem).wait()

    to_mate = remote(t_ref.at[pl.ds(8 * (1 - zh), 8)], mate_ref, mate_sem.at[0], mate_sem.at[1], mate_dev)

    def chunk_of(src_z):
        src_z = (src_z + 32) % 16
        return (((src_z % 8) // 2) * 2 + src_z // 8) * 2 + c

    own_chunk = chunk_of(z)
    for step in (3, 13, 0):
        for u in range(8):
            target = (u // 2) * 4 + 2 * (u % 2) + k % 2
            recv = piv_recv.at[{3: 3, 13: 13, 0: 0}[step]]
            tile = remote(t_ref.at[u], piv_ref.at[own_chunk, yx], piv_send.at[0], recv, z_dev(z + step, target, c))
            if step:
                tile.start()
                continue

            @pl.when(target == yx)
            def _():
                pltpu.make_async_copy(t_ref.at[u], piv_ref.at[own_chunk, yx], recv).start()

            @pl.when(target != yx)
            def _():
                tile.start()

    def send_rows(src_ref, base, slot):
        for yx2, c2 in plane_peers(yx, c):
            remote(src_ref.at[pl.ds(base + 4 * c2, 4)], rows_ref.at[slot], row_send.at[0], row_recv.at[0],
                   dev(k, yx2, zh, c2)).start()

        pltpu.make_async_copy(src_ref.at[pl.ds(base + 4 * c, 4)], rows_ref.at[slot], row_recv.at[0]).start()

    def piv_copy(chunk, target, send, recv):
        return remote(piv_ref.at[chunk], piv_ref.at[chunk], send, recv, target)

    def sib_copy(chunk):
        return piv_copy(chunk, sib_dev, sib_send.at[0], sib_recv.at[0])

    def hop(off, step):
        return piv_copy(chunk_of(z - off), z_dev(z + 16 + step, yx, c), hop_send.at[0], piv_recv.at[(off + step) % 16])

    def arrived(off, steps=()):
        drain(piv_ref.at[chunk_of(z - off)], piv_recv.at[off % 16])
        for step in steps:
            hop(off, step).start()
        sib_copy(chunk_of(z - off)).start()

    to_mate.start()
    send_rows(t_ref, 8 * zh, (zh * 2 + c) * 16 + yx)

    @pl.when(away == 0)
    def _():
        arrived(0, (1, -1))

    @pl.when(away == 1)
    def _():
        arrived(3, (3, 1, -1))
        arrived(-3, (-3, -1, 1))

    to_mate.wait_recv()
    send_rows(mate_ref, 0, ((1 - zh) * 2 + c) * 16 + yx)

    @pl.when(away == 0)
    def _():
        arrived(6, (2, 1, -1))
        arrived(-6, (-1, 1))
        for off in (2, -2, 4, -4, 8):
            arrived(off)

    @pl.when(away == 1)
    def _():
        for off in (1, -1, 5, -5, 7, -7):
            arrived(off)

    drain(rows_ref, row_recv.at[0])
    split_rows(rows_ref, ag, ax)
    drain(piv_ref.at[pl.ds(0, 8)], sib_recv.at[0])
    block(piv_ref, part_ref, ag, ax, bg, bx, gg, xx, yx)

    slot = c * 16 + yx

    for yx2, c2 in plane_peers(yx, c):
        remote(part_ref, parts.at[slot], send1.at[0], recv1.at[0], dev(k, yx2, zh, c2)).start()

    pltpu.make_async_copy(part_ref, parts.at[slot], recv1.at[0]).start()
    drain(parts, recv1.at[0])
    for c2 in range(2):
        plane_rows[pl.ds(c2 * 8, 8), :] = jnp.sum(parts[pl.ds(c2 * 16, 16)], axis=0)

    @pl.when(zh == 0)
    def _():
        @pl.loop(1, 16)
        def _(i):
            remote(plane_rows, out_ref.at[k], send2.at[0], recv2.at[0], z_dev(z + far_first(i), yx, c)).start()

        pltpu.make_async_copy(plane_rows, out_ref.at[k], recv2.at[0]).start()

    @pl.when(zh == 1)
    def _():
        remote(plane_rows, out_ref.at[8], send2.at[0], recv3.at[0], mate_dev).start()
        pltpu.make_async_copy(plane_rows, out_ref.at[8], recv3.at[0]).start()

    to_mate.wait_send()

    @pl.when(away == 0)
    def _():
        drain(rows_ref.at[pl.ds(0, 5)], piv_send.at[0])
        drain(rows_ref.at[pl.ds(0, 3), pl.ds(0, 1)], piv_send.at[0])
        drain(piv_ref.at[pl.ds(0, 7)], hop_send.at[0])

    @pl.when(away == 1)
    def _():
        drain(rows_ref.at[pl.ds(0, 6)], piv_send.at[0])
        drain(piv_ref.at[pl.ds(0, 6)], hop_send.at[0])

    drain(rows_ref.at[pl.ds(0, 62)], row_send.at[0])
    drain(piv_ref.at[pl.ds(0, 8)], sib_send.at[0])
    drain(out_ref.at[pl.ds(0, 8)], recv2.at[0])
    drain(out_ref.at[8], recv3.at[0])
    factor(out_ref, ridge_ref, both_ref.at[0], both_ref.at[1], f_ref, k)
    drain(parts.at[pl.ds(0, 31)], send1.at[0])

    @pl.when(zh == 0)
    def _():
        drain(parts.at[pl.ds(0, 30)], send2.at[0])

    @pl.when(zh == 1)
    def _():
        drain(plane_rows, send2.at[0])


def panel(order, x, g, ridge):
    dma = pltpu.SemaphoreType.DMA
    return pl.pallas_call(
        panel_kernel,
        out_shape=jax.ShapeDtypeStruct((2, 32, 128), F32),
        in_specs=[HBM] * 4,
        out_specs=VM,
        scratch_shapes=[
            pltpu.VMEM((9, 16, 128), F32),
            pltpu.VMEM((128, 128), F32),
            pltpu.VMEM((1, 128), F32),
            pltpu.SMEM((1, 32), jnp.int32),
            pltpu.VMEM((49, 8, 32), BF16),
            pltpu.VMEM((32, 8, 49), BF16),
            pltpu.VMEM((128, 49), F32),
            pltpu.VMEM((128, 49), F32),
            pltpu.VMEM((16, 8, 128), F32),
            pltpu.VMEM((16, 16, 128), BF16),
            pltpu.VMEM((8, 16, 128), BF16),
            pltpu.VMEM((64, 4, 16, 128), BF16),
            pltpu.VMEM((16, 16, 16, 128), BF16),
        ]
        + [pltpu.VMEM((512, 512), BF16)] * 4
        + [pltpu.VMEM((512, 512), F32)] * 2
        + [pltpu.VMEM((8, 128), F32), pltpu.VMEM((32, 8, 128), F32), pltpu.VMEM((16, 128), F32)]
        + [dma((n,)) for n in (2, 1, 1, 1, 16, 1, 4, 1, 1, 1, 1, 1, 1, 1)],
        compiler_params=pltpu.CompilerParams(
            collective_id=0, has_side_effects=True, vmem_limit_bytes=56 * 1024 * 1024),
        name="panel",
    )(order, x, g, ridge)


def local(activations, cotangents, ordering, ridge):
    x = activations.transpose(1, 2, 3, 0).reshape(49, 8, 32)
    both = panel(ordering, x, cotangents, ridge.reshape(1, 128))
    return both[0], both[1]


def solution(mesh):
    return jax.shard_map(
        local,
        mesh=mesh,
        in_specs=(P("rows", None, None, "chan"), P("rows", "chan", None), P("rows", None), P()),
        out_specs=(P("rows", None), P("rows", None)),
        check_vma=False,
    )
```

```python
import jax
import jax.numpy as jnp
from jax import lax
from jax.experimental import pallas as pl
from jax.experimental.pallas import tpu as pltpu
from jax.sharding import PartitionSpec as P

F32 = jnp.float32
BF16 = jnp.bfloat16
MESH = pl.DeviceIdType.MESH
VM = pl.BlockSpec(memory_space=pltpu.VMEM)
HBM = pl.BlockSpec(memory_space=pltpu.HBM)


def place():
    k = lax.axis_index("rows")
    j = lax.axis_index("chan")
    return k, j // 4, (j // 2) % 2, j % 2


def dev(k, yx, zh, c):
    return {"rows": k, "chan": (yx * 2 + zh) * 2 + c}


def plane_peers(yx, c):
    steps = sorted(((dy, dx) for dy in range(4) for dx in range(4)),
                   key=lambda step: -sum(min(d, 4 - d) for d in step))
    for dy, dx in steps:
        for flip in (0, 1):
            if dy or dx or flip:
                yield ((yx // 4 + dy) % 4) * 4 + (yx + dx) % 4, (c + flip) % 2


def far_first(i):
    return 8 + (i // 2) * (1 - 2 * (i % 2))


def z_dev(z, yx, c):
    z = z % 16
    return dev(z % 8, yx, z // 8, c)


def lay_out(order_ref, x_ref, g_ref, out_ref, ge, go, xs, c):
    pos = lax.broadcasted_iota(jnp.int32, (49, 128), 0)
    lane = lax.broadcasted_iota(jnp.int32, (49, 128), 1)
    slot = (pos // 7) * 8 + pos % 7
    low = jnp.where(lane == slot, 1.0, 0.0).astype(BF16)
    high = jnp.where(lane == slot + 64, 1.0, 0.0).astype(BF16)
    for u in range(16):
        ge[pl.ds(u * 8, 8), :] = g_ref[order_ref[0, 2 * u]].astype(F32)
        go[pl.ds(u * 8, 8), :] = g_ref[order_ref[0, 2 * u + 1]].astype(F32)
    grads = jnp.dot(ge[...].astype(BF16), low, preferred_element_type=F32) + jnp.dot(
        go[...].astype(BF16), high, preferred_element_type=F32
    )
    grads = grads.reshape(16, 8, 128)
    unit = lax.broadcasted_iota(jnp.int32, (16, 32), 0)
    example = lax.broadcasted_iota(jnp.int32, (16, 32), 1)
    even = jnp.zeros((16, 32), F32)
    odd = jnp.zeros((16, 32), F32)
    for u in range(16):
        even = jnp.where((unit == u) & (example == order_ref[0, 2 * u]), 1.0, even)
        odd = jnp.where((unit == u) & (example == order_ref[0, 2 * u + 1]), 1.0, odd)
    even = even.astype(BF16)
    odd = odd.astype(BF16)
    for ch in range(8):
        part = x_ref[:, ch, :]
        dims = (((0,), (0,)), ((), ()))
        at_low = lax.dot_general(part, low, dims, preferred_element_type=F32).astype(BF16)
        at_high = lax.dot_general(part, high, dims, preferred_element_type=F32).astype(BF16)
        xs[:, ch, :] = jnp.dot(even, at_low, preferred_element_type=F32) + jnp.dot(
            odd, at_high, preferred_element_type=F32
        )
    inputs = xs[...]
    first = jnp.where(c == 0, grads, inputs)
    second = jnp.where(c == 0, inputs, grads)
    out_ref[...] = jnp.concatenate([first, second], axis=1).astype(BF16)


def split(z2, u, even, odd, grads, inputs):
    mask = lax.broadcasted_iota(jnp.int32, (16, 16, 128), 1) < 8
    at = pl.ds(z2 * 256, 256), pl.ds(u * 128, 128)
    grads[at] = jnp.where(mask, even, odd).reshape(256, 128)
    inputs[at] = jnp.where(mask, odd, even).reshape(256, 128)


def split_rows(rows_ref, ag, ax):
    for z2 in range(2):
        for u in range(4):
            split(z2, u, rows_ref[pl.ds(z2 * 32, 16), u], rows_ref[pl.ds(z2 * 32 + 16, 16), u], ag, ax)


def block(piv_ref, out_ref, ag, ax, bg, bx, gg, xx, yx):
    for z2 in range(2):
        for u in range(4):
            chunk = (u * 2 + z2) * 2
            split(z2, u, piv_ref[chunk], piv_ref[chunk + 1], bg, bx)
    dims = (((0,), (0,)), ((), ()))
    gg[...] = lax.dot_general(ag[...], bg[...], dims, preferred_element_type=F32)
    xx[...] = lax.dot_general(ax[...], bx[...], dims, preferred_element_type=F32)
    lanes = lax.broadcasted_iota(jnp.int32, (128, 128), 0)
    cols = lax.broadcasted_iota(jnp.int32, (128, 128), 1)
    piv0 = 16 * (yx % 2) + 2 * ((yx // 4) * 2 + (yx % 4) // 2)
    pieces = jnp.zeros((8, 128), F32)
    for t in range(4):
        col = pl.ds(t * 128, 128)
        summed = []
        for e in range(8):
            wide = xx[pl.ds(e * 64, 64), col]
            wide = (
                wide
                + pltpu.roll(pltpu.roll(wide, 1, 0), 1, 1)
                + pltpu.roll(pltpu.roll(wide, 63, 0), 127, 1)
            )
            wide = (
                wide
                + pltpu.roll(pltpu.roll(wide, 8, 0), 8, 1)
                + pltpu.roll(pltpu.roll(wide, 56, 0), 120, 1)
            )
            summed.append(jnp.sum(gg[pl.ds(e * 64, 64), col] * wide, axis=0, keepdims=True))
        folded = jnp.concatenate(summed, axis=0)
        spread = jnp.where(cols == piv0 + 32 * t + lanes // 64, 1.0, 0.0)
        pieces = pieces + jnp.dot(folded, spread, precision=lax.Precision.HIGHEST, preferred_element_type=F32)
    out_ref[...] = pieces


def eliminate(left, right, store):
    full = (8, 128)
    for m0 in range(16):
        j0 = 8 * m0
        rows = [jnp.broadcast_to(left[m0][i:i + 1, :], full) for i in range(8)]
        rights = [jnp.broadcast_to(right[m0][i:i + 1, :], full) for i in range(8)]
        cols = [jnp.broadcast_to(left[m0][:, j0 + l:j0 + l + 1], full) for l in range(8)]
        e = [[jnp.broadcast_to(cols[l][i:i + 1, :], full) if i <= l else None for l in range(8)] for i in range(8)]
        inverse, ratio = [], {}
        for i in range(8):
            if i % 2 == 0:
                inverse.append(1.0 / e[i][i])
                inverse.append(e[i][i] / (e[i][i] * e[i + 1][i + 1] - e[i][i + 1] * e[i][i + 1]))
            for l in range(i + 1, 8):
                ratio[i, l] = e[i][l] * inverse[i]
            for l in range(i + 1, 8):
                for n in range(l, 8):
                    e[l][n] = e[l][n] - ratio[i, l] * e[i][n]
                rows[l] = rows[l] - ratio[i, l] * rows[i]
                rights[l] = rights[l] - ratio[i, l] * rights[i]
        for i in range(8):
            store(j0 + i, rights[i] * lax.rsqrt(e[i][i]))
        if m0 == 15:
            break
        for i in reversed(range(8)):
            rows[i] = rows[i] * inverse[i]
            rights[i] = rights[i] * inverse[i]
            for l in reversed(range(i + 1, 8)):
                rows[i] = rows[i] - ratio[i, l] * rows[l]
                rights[i] = rights[i] - ratio[i, l] * rights[l]
        for m in range(m0 + 1, 16):
            factors = [jnp.broadcast_to(left[m][:, j0 + i:j0 + i + 1], full) for i in range(8)]
            for side, vectors in ((left, rows), (right, rights)):
                terms = [f * v for f, v in zip(factors, vectors)]
                while len(terms) > 1:
                    terms = [terms[n] + terms[n + 1] for n in range(0, len(terms), 2)]
                side[m] = side[m] - terms[0]


def factor(panel_ref, ridge_ref, gram_ref, factor_ref, f_ref, k):
    gram_ref[pl.ds(0, 16), :] = panel_ref[k]
    gram_ref[pl.ds(16, 16), :] = panel_ref[8]
    gram = gram_ref[...]
    diag = panel_ref[0:8].reshape(128, 128)
    row = lax.broadcasted_iota(jnp.int32, (128, 128), 0)
    col = lax.broadcasted_iota(jnp.int32, (128, 128), 1)
    system = 0.5 * (diag + diag.T) + jnp.where(row == col, ridge_ref[...], 0.0)
    right = jnp.concatenate([gram, jnp.zeros((96, 128), F32)], axis=0).T
    left = [system[8 * m:8 * m + 8] for m in range(16)]
    right = [right[8 * m:8 * m + 8] for m in range(16)]

    def store(row, values):
        f_ref[pl.ds(row, 1), :] = values[0:1]

    eliminate(left, right, store)
    factor_ref[...] = f_ref[...].T[:32]


def panel_kernel(order_hbm, x_hbm, g_hbm, ridge_hbm, both_ref,
                 out_ref, f_ref, ridge_ref, order_ref, x_ref, g_ref, ge, go, xs, t_ref, mate_ref, rows_ref, piv_ref, ag, ax, bg, bx, gg, xx, part_ref, parts, plane_rows,
                 mate_sem, row_send, row_recv, piv_send, piv_recv, hop_send, in_sem,
                 sib_send, sib_recv, send1, recv1, send2, recv2, recv3):
    k, yx, zh, c = place()
    z = zh * 8 + k
    away = (k + yx) % 2
    mate_dev = dev(k, yx, 1 - zh, c)
    sib_dev = dev(k, yx, zh, 1 - c)

    barrier = pltpu.get_barrier_semaphore()

    def signal(target):
        pl.semaphore_signal(barrier, inc=1, device_id=target, device_id_type=MESH)

    @pl.loop(1, 16)
    def _(i):
        signal(z_dev(z + far_first(i), yx, c))

    @pl.when(away == 1)
    def _():
        @pl.loop(0, 16)
        def _(i):
            signal(z_dev(z + 3, i, c))
            signal(z_dev(z + 13, i, c))

    operands = [
        pltpu.make_async_copy(src, dst, in_sem.at[n])
        for n, (src, dst) in enumerate(((order_hbm, order_ref), (x_hbm, x_ref), (g_hbm, g_ref), (ridge_hbm, ridge_ref)))
    ]
    for copy in operands:
        copy.start()

    for yx2, c2 in plane_peers(yx, c):
        signal(dev(k, yx2, zh, c2))

    for copy in operands:
        copy.wait()
    lay_out(order_ref, x_ref, g_ref, t_ref, ge, go, xs, c)
    pl.semaphore_wait(barrier, 62)

    def remote(src, dst, send, recv, target):
        return pltpu.make_async_remote_copy(
            src_ref=src, dst_ref=dst, send_sem=send, recv_sem=recv, device_id=target, device_id_type=MESH)

    def drain(ref, sem):
        pltpu.make_async_copy(ref, ref, sem).wait()

    to_mate = remote(t_ref.at[pl.ds(8 * (1 - zh), 8)], mate_ref, mate_sem.at[0], mate_sem.at[1], mate_dev)

    def chunk_of(src_z):
        src_z = (src_z + 32) % 16
        return (((src_z % 8) // 2) * 2 + src_z // 8) * 2 + c

    own_chunk = chunk_of(z)
    for step in (3, 13, 0):
        for u in range(8):
            target = (u // 2) * 4 + 2 * (u % 2) + k % 2
            recv = piv_recv.at[{3: 3, 13: 13, 0: 0}[step]]
            tile = remote(t_ref.at[u], piv_ref.at[own_chunk, yx], piv_send.at[0], recv, z_dev(z + step, target, c))
            if step:
                tile.start()
                continue

            @pl.when(target == yx)
            def _():
                pltpu.make_async_copy(t_ref.at[u], piv_ref.at[own_chunk, yx], recv).start()

            @pl.when(target != yx)
            def _():
                tile.start()

    def send_rows(src_ref, base, slot):
        for yx2, c2 in plane_peers(yx, c):
            remote(src_ref.at[pl.ds(base + 4 * c2, 4)], rows_ref.at[slot], row_send.at[0], row_recv.at[0],
                   dev(k, yx2, zh, c2)).start()

        pltpu.make_async_copy(src_ref.at[pl.ds(base + 4 * c, 4)], rows_ref.at[slot], row_recv.at[0]).start()

    def piv_copy(chunk, target, send, recv):
        return remote(piv_ref.at[chunk], piv_ref.at[chunk], send, recv, target)

    def sib_copy(chunk):
        return piv_copy(chunk, sib_dev, sib_send.at[0], sib_recv.at[0])

    def hop(off, step):
        return piv_copy(chunk_of(z - off), z_dev(z + 16 + step, yx, c), hop_send.at[0], piv_recv.at[(off + step) % 16])

    def arrived(off, steps=()):
        drain(piv_ref.at[chunk_of(z - off)], piv_recv.at[off % 16])
        for step in steps:
            hop(off, step).start()
        sib_copy(chunk_of(z - off)).start()

    to_mate.start()
    send_rows(t_ref, 8 * zh, (zh * 2 + c) * 16 + yx)

    @pl.when(away == 0)
    def _():
        arrived(0, (1, -1))

    @pl.when(away == 1)
    def _():
        arrived(3, (3, 1, -1))
        arrived(-3, (-3, -1, 1))

    to_mate.wait_recv()
    send_rows(mate_ref, 0, ((1 - zh) * 2 + c) * 16 + yx)

    @pl.when(away == 0)
    def _():
        arrived(6, (2, 1, -1))
        arrived(-6, (-1, 1))
        for off in (2, -2, 4, -4, 8):
            arrived(off)

    @pl.when(away == 1)
    def _():
        for off in (1, -1, 5, -5, 7, -7):
            arrived(off)

    drain(rows_ref, row_recv.at[0])
    split_rows(rows_ref, ag, ax)
    drain(piv_ref.at[pl.ds(0, 8)], sib_recv.at[0])
    block(piv_ref, part_ref, ag, ax, bg, bx, gg, xx, yx)

    slot = c * 16 + yx

    for yx2, c2 in plane_peers(yx, c):
        remote(part_ref, parts.at[slot], send1.at[0], recv1.at[0], dev(k, yx2, zh, c2)).start()

    pltpu.make_async_copy(part_ref, parts.at[slot], recv1.at[0]).start()
    drain(parts, recv1.at[0])
    for c2 in range(2):
        plane_rows[pl.ds(c2 * 8, 8), :] = jnp.sum(parts[pl.ds(c2 * 16, 16)], axis=0)

    @pl.when(zh == 0)
    def _():
        @pl.loop(1, 16)
        def _(i):
            remote(plane_rows, out_ref.at[k], send2.at[0], recv2.at[0], z_dev(z + far_first(i), yx, c)).start()

        pltpu.make_async_copy(plane_rows, out_ref.at[k], recv2.at[0]).start()

    @pl.when(zh == 1)
    def _():
        remote(plane_rows, out_ref.at[8], send2.at[0], recv3.at[0], mate_dev).start()
        pltpu.make_async_copy(plane_rows, out_ref.at[8], recv3.at[0]).start()

    to_mate.wait_send()

    @pl.when(away == 0)
    def _():
        drain(rows_ref.at[pl.ds(0, 5)], piv_send.at[0])
        drain(rows_ref.at[pl.ds(0, 3), pl.ds(0, 1)], piv_send.at[0])
        drain(piv_ref.at[pl.ds(0, 7)], hop_send.at[0])

    @pl.when(away == 1)
    def _():
        drain(rows_ref.at[pl.ds(0, 6)], piv_send.at[0])
        drain(piv_ref.at[pl.ds(0, 6)], hop_send.at[0])

    drain(rows_ref.at[pl.ds(0, 62)], row_send.at[0])
    drain(piv_ref.at[pl.ds(0, 8)], sib_send.at[0])
    drain(out_ref.at[pl.ds(0, 8)], recv2.at[0])
    drain(out_ref.at[8], recv3.at[0])
    factor(out_ref, ridge_ref, both_ref.at[0], both_ref.at[1], f_ref, k)
    drain(parts.at[pl.ds(0, 31)], send1.at[0])

    @pl.when(zh == 0)
    def _():
        drain(parts.at[pl.ds(0, 30)], send2.at[0])

    @pl.when(zh == 1)
    def _():
        drain(plane_rows, send2.at[0])


def panel(order, x, g, ridge):
    dma = pltpu.SemaphoreType.DMA
    return pl.pallas_call(
        panel_kernel,
        out_shape=jax.ShapeDtypeStruct((2, 32, 128), F32),
        in_specs=[HBM] * 4,
        out_specs=VM,
        scratch_shapes=[
            pltpu.VMEM((9, 16, 128), F32),
            pltpu.VMEM((128, 128), F32),
            pltpu.VMEM((1, 128), F32),
            pltpu.SMEM((1, 32), jnp.int32),
            pltpu.VMEM((49, 8, 32), BF16),
            pltpu.VMEM((32, 8, 49), BF16),
            pltpu.VMEM((128, 49), F32),
            pltpu.VMEM((128, 49), F32),
            pltpu.VMEM((16, 8, 128), F32),
            pltpu.VMEM((16, 16, 128), BF16),
            pltpu.VMEM((8, 16, 128), BF16),
            pltpu.VMEM((64, 4, 16, 128), BF16),
            pltpu.VMEM((16, 16, 16, 128), BF16),
        ]
        + [pltpu.VMEM((512, 512), BF16)] * 4
        + [pltpu.VMEM((512, 512), F32)] * 2
        + [pltpu.VMEM((8, 128), F32), pltpu.VMEM((32, 8, 128), F32), pltpu.VMEM((16, 128), F32)]
        + [dma((n,)) for n in (2, 1, 1, 1, 16, 1, 4, 1, 1, 1, 1, 1, 1, 1)],
        compiler_params=pltpu.CompilerParams(
            collective_id=0, has_side_effects=True, vmem_limit_bytes=56 * 1024 * 1024),
        name="panel",
    )(order, x, g, ridge)


def local(activations, cotangents, ordering, ridge):
    x = activations.transpose(1, 2, 3, 0).reshape(49, 8, 32)
    both = panel(ordering, x, cotangents, ridge.reshape(1, 128))
    return both[0], both[1]


def solution(mesh):
    return jax.shard_map(
        local,
        mesh=mesh,
        in_specs=(P("rows", None, None, "chan"), P("rows", "chan", None), P("rows", None), P()),
        out_specs=(P("rows", None), P("rows", None)),
        check_vma=False,
    )
```

```python
import jax
import jax.numpy as jnp
from jax import lax
from jax.experimental import pallas as pl
from jax.experimental.pallas import tpu as pltpu
from jax.sharding import PartitionSpec as P

F32 = jnp.float32
BF16 = jnp.bfloat16
MESH = pl.DeviceIdType.MESH
VM = pl.BlockSpec(memory_space=pltpu.VMEM)
HBM = pl.BlockSpec(memory_space=pltpu.HBM)


def place():
    k = lax.axis_index("rows")
    j = lax.axis_index("chan")
    return k, j // 4, (j // 2) % 2, j % 2


def dev(k, yx, zh, c):
    return {"rows": k, "chan": (yx * 2 + zh) * 2 + c}


def plane_peers(yx, c):
    steps = sorted(((dy, dx) for dy in range(4) for dx in range(4)),
                   key=lambda step: -sum(min(d, 4 - d) for d in step))
    for dy, dx in steps:
        for flip in (0, 1):
            if dy or dx or flip:
                yield ((yx // 4 + dy) % 4) * 4 + (yx + dx) % 4, (c + flip) % 2


def far_first(i):
    return 8 + (i // 2) * (1 - 2 * (i % 2))


def z_dev(z, yx, c):
    z = z % 16
    return dev(z % 8, yx, z // 8, c)


def lay_out(order_ref, x_ref, g_ref, out_ref, ge, go, xs, c):
    pos = lax.broadcasted_iota(jnp.int32, (49, 128), 0)
    lane = lax.broadcasted_iota(jnp.int32, (49, 128), 1)
    slot = (pos // 7) * 8 + pos % 7
    low = jnp.where(lane == slot, 1.0, 0.0).astype(BF16)
    high = jnp.where(lane == slot + 64, 1.0, 0.0).astype(BF16)
    for u in range(16):
        ge[pl.ds(u * 8, 8), :] = g_ref[order_ref[0, 2 * u]].astype(F32)
        go[pl.ds(u * 8, 8), :] = g_ref[order_ref[0, 2 * u + 1]].astype(F32)
    grads = jnp.dot(ge[...].astype(BF16), low, preferred_element_type=F32) + jnp.dot(
        go[...].astype(BF16), high, preferred_element_type=F32
    )
    grads = grads.reshape(16, 8, 128)
    unit = lax.broadcasted_iota(jnp.int32, (16, 32), 0)
    example = lax.broadcasted_iota(jnp.int32, (16, 32), 1)
    even = jnp.zeros((16, 32), F32)
    odd = jnp.zeros((16, 32), F32)
    for u in range(16):
        even = jnp.where((unit == u) & (example == order_ref[0, 2 * u]), 1.0, even)
        odd = jnp.where((unit == u) & (example == order_ref[0, 2 * u + 1]), 1.0, odd)
    even = even.astype(BF16)
    odd = odd.astype(BF16)
    for ch in range(8):
        part = x_ref[:, ch, :]
        dims = (((0,), (0,)), ((), ()))
        at_low = lax.dot_general(part, low, dims, preferred_element_type=F32).astype(BF16)
        at_high = lax.dot_general(part, high, dims, preferred_element_type=F32).astype(BF16)
        xs[:, ch, :] = jnp.dot(even, at_low, preferred_element_type=F32) + jnp.dot(
            odd, at_high, preferred_element_type=F32
        )
    inputs = xs[...]
    first = jnp.where(c == 0, grads, inputs)
    second = jnp.where(c == 0, inputs, grads)
    out_ref[...] = jnp.concatenate([first, second], axis=1).astype(BF16)


def split(z2, u, even, odd, grads, inputs):
    mask = lax.broadcasted_iota(jnp.int32, (16, 16, 128), 1) < 8
    at = pl.ds(z2 * 256, 256), pl.ds(u * 128, 128)
    grads[at] = jnp.where(mask, even, odd).reshape(256, 128)
    inputs[at] = jnp.where(mask, odd, even).reshape(256, 128)


def split_rows(rows_ref, ag, ax):
    for z2 in range(2):
        for u in range(4):
            split(z2, u, rows_ref[pl.ds(z2 * 32, 16), u], rows_ref[pl.ds(z2 * 32 + 16, 16), u], ag, ax)


def block(piv_ref, out_ref, ag, ax, bg, bx, gg, xx, yx):
    for z2 in range(2):
        for u in range(4):
            chunk = (u * 2 + z2) * 2
            split(z2, u, piv_ref[chunk], piv_ref[chunk + 1], bg, bx)
    dims = (((0,), (0,)), ((), ()))
    gg[...] = lax.dot_general(ag[...], bg[...], dims, preferred_element_type=F32)
    xx[...] = lax.dot_general(ax[...], bx[...], dims, preferred_element_type=F32)
    lanes = lax.broadcasted_iota(jnp.int32, (128, 128), 0)
    cols = lax.broadcasted_iota(jnp.int32, (128, 128), 1)
    piv0 = 16 * (yx % 2) + 2 * ((yx // 4) * 2 + (yx % 4) // 2)
    pieces = jnp.zeros((8, 128), F32)
    for t in range(4):
        col = pl.ds(t * 128, 128)
        summed = []
        for e in range(8):
            wide = xx[pl.ds(e * 64, 64), col]
            wide = (
                wide
                + pltpu.roll(pltpu.roll(wide, 1, 0), 1, 1)
                + pltpu.roll(pltpu.roll(wide, 63, 0), 127, 1)
            )
            wide = (
                wide
                + pltpu.roll(pltpu.roll(wide, 8, 0), 8, 1)
                + pltpu.roll(pltpu.roll(wide, 56, 0), 120, 1)
            )
            summed.append(jnp.sum(gg[pl.ds(e * 64, 64), col] * wide, axis=0, keepdims=True))
        folded = jnp.concatenate(summed, axis=0)
        spread = jnp.where(cols == piv0 + 32 * t + lanes // 64, 1.0, 0.0)
        pieces = pieces + jnp.dot(folded, spread, precision=lax.Precision.HIGHEST, preferred_element_type=F32)
    out_ref[...] = pieces


def eliminate(left, right, store):
    full = (8, 128)
    for m0 in range(16):
        j0 = 8 * m0
        rows = [jnp.broadcast_to(left[m0][i:i + 1, :], full) for i in range(8)]
        rights = [jnp.broadcast_to(right[m0][i:i + 1, :], full) for i in range(8)]
        cols = [jnp.broadcast_to(left[m0][:, j0 + l:j0 + l + 1], full) for l in range(8)]
        e = [[jnp.broadcast_to(cols[l][i:i + 1, :], full) if i <= l else None for l in range(8)] for i in range(8)]
        inverse, ratio, unit = [], {}, {}
        for i in range(8):
            if i % 2 == 0:
                inverse.append(1.0 / e[i][i])
                inverse.append(e[i][i] / (e[i][i] * e[i + 1][i + 1] - e[i][i + 1] * e[i][i + 1]))
            for l in range(i + 1, 8):
                ratio[i, l] = e[i][l] * inverse[i]
            for l in range(i + 1, 8):
                for n in range(l, 8):
                    e[l][n] = e[l][n] - ratio[i, l] * e[i][n]
                unit[l, i] = -ratio[i, l]
                for n in range(i):
                    unit[l, n] = unit[l, n] - ratio[i, l] * unit[i, n]
                rows[l] = rows[l] - ratio[i, l] * rows[i]
                rights[l] = rights[l] - ratio[i, l] * rights[i]
        for i in range(8):
            store(j0 + i, rights[i] * lax.rsqrt(e[i][i]))
        if m0 == 15:
            break
        rows = [row * scale for row, scale in zip(rows, inverse)]
        rights = [row * scale for row, scale in zip(rights, inverse)]

        def back(vectors, i):
            terms = [vectors[i]] + [unit[l, i] * vectors[l] for l in range(i + 1, 8)]
            while len(terms) > 1:
                terms = [sum(terms[n + 1:n + 2], terms[n]) for n in range(0, len(terms), 2)]
            return terms[0]

        rows = [back(rows, i) for i in range(8)]
        rights = [back(rights, i) for i in range(8)]
        for m in range(m0 + 1, 16):
            factors = [jnp.broadcast_to(left[m][:, j0 + i:j0 + i + 1], full) for i in range(8)]
            for side, vectors in ((left, rows), (right, rights)):
                terms = [f * v for f, v in zip(factors, vectors)]
                while len(terms) > 1:
                    terms = [terms[n] + terms[n + 1] for n in range(0, len(terms), 2)]
                side[m] = side[m] - terms[0]


def factor(panel_ref, ridge_ref, gram_ref, factor_ref, f_ref, k):
    gram_ref[pl.ds(0, 16), :] = panel_ref[k]
    gram_ref[pl.ds(16, 16), :] = panel_ref[8]
    gram = gram_ref[...]
    diag = panel_ref[0:8].reshape(128, 128)
    row = lax.broadcasted_iota(jnp.int32, (128, 128), 0)
    col = lax.broadcasted_iota(jnp.int32, (128, 128), 1)
    system = 0.5 * (diag + diag.T) + jnp.where(row == col, ridge_ref[...], 0.0)
    right = jnp.concatenate([gram, jnp.zeros((96, 128), F32)], axis=0).T
    left = [system[8 * m:8 * m + 8] for m in range(16)]
    right = [right[8 * m:8 * m + 8] for m in range(16)]

    def store(row, values):
        f_ref[pl.ds(row, 1), :] = values[0:1]

    eliminate(left, right, store)
    factor_ref[...] = f_ref[...].T[:32]


def panel_kernel(order_hbm, x_hbm, g_hbm, ridge_hbm, both_ref,
                 out_ref, f_ref, ridge_ref, order_ref, x_ref, g_ref, ge, go, xs, t_ref, mate_ref, rows_ref, piv_ref, ag, ax, bg, bx, gg, xx, part_ref, parts, plane_rows,
                 mate_sem, row_send, row_recv, piv_send, piv_recv, hop_send, in_sem,
                 sib_send, sib_recv, send1, recv1, send2, recv2, recv3):
    k, yx, zh, c = place()
    z = zh * 8 + k
    away = (k + yx) % 2
    mate_dev = dev(k, yx, 1 - zh, c)
    sib_dev = dev(k, yx, zh, 1 - c)

    barrier = pltpu.get_barrier_semaphore()

    def signal(target):
        pl.semaphore_signal(barrier, inc=1, device_id=target, device_id_type=MESH)

    @pl.loop(1, 16)
    def _(i):
        signal(z_dev(z + far_first(i), yx, c))

    @pl.when(away == 1)
    def _():
        @pl.loop(0, 16)
        def _(i):
            signal(z_dev(z + 3, i, c))
            signal(z_dev(z + 13, i, c))

    operands = [
        pltpu.make_async_copy(src, dst, in_sem.at[n])
        for n, (src, dst) in enumerate(((order_hbm, order_ref), (x_hbm, x_ref), (g_hbm, g_ref), (ridge_hbm, ridge_ref)))
    ]
    for copy in operands:
        copy.start()

    for yx2, c2 in plane_peers(yx, c):
        signal(dev(k, yx2, zh, c2))

    for copy in operands:
        copy.wait()
    lay_out(order_ref, x_ref, g_ref, t_ref, ge, go, xs, c)
    pl.semaphore_wait(barrier, 62)

    def remote(src, dst, send, recv, target):
        return pltpu.make_async_remote_copy(
            src_ref=src, dst_ref=dst, send_sem=send, recv_sem=recv, device_id=target, device_id_type=MESH)

    def drain(ref, sem):
        pltpu.make_async_copy(ref, ref, sem).wait()

    to_mate = remote(t_ref.at[pl.ds(8 * (1 - zh), 8)], mate_ref, mate_sem.at[0], mate_sem.at[1], mate_dev)

    def chunk_of(src_z):
        src_z = (src_z + 32) % 16
        return (((src_z % 8) // 2) * 2 + src_z // 8) * 2 + c

    own_chunk = chunk_of(z)
    for step in (3, 13, 0):
        for u in range(8):
            target = (u // 2) * 4 + 2 * (u % 2) + k % 2
            recv = piv_recv.at[{3: 3, 13: 13, 0: 0}[step]]
            tile = remote(t_ref.at[u], piv_ref.at[own_chunk, yx], piv_send.at[0], recv, z_dev(z + step, target, c))
            if step:
                tile.start()
                continue

            @pl.when(target == yx)
            def _():
                pltpu.make_async_copy(t_ref.at[u], piv_ref.at[own_chunk, yx], recv).start()

            @pl.when(target != yx)
            def _():
                tile.start()

    def send_rows(src_ref, base, slot):
        for yx2, c2 in plane_peers(yx, c):
            remote(src_ref.at[pl.ds(base + 4 * c2, 4)], rows_ref.at[slot], row_send.at[0], row_recv.at[0],
                   dev(k, yx2, zh, c2)).start()

        pltpu.make_async_copy(src_ref.at[pl.ds(base + 4 * c, 4)], rows_ref.at[slot], row_recv.at[0]).start()

    def piv_copy(chunk, target, send, recv):
        return remote(piv_ref.at[chunk], piv_ref.at[chunk], send, recv, target)

    def sib_copy(chunk):
        return piv_copy(chunk, sib_dev, sib_send.at[0], sib_recv.at[0])

    def hop(off, step):
        return piv_copy(chunk_of(z - off), z_dev(z + 16 + step, yx, c), hop_send.at[0], piv_recv.at[(off + step) % 16])

    def arrived(off, steps=()):
        drain(piv_ref.at[chunk_of(z - off)], piv_recv.at[off % 16])
        for step in steps:
            hop(off, step).start()
        sib_copy(chunk_of(z - off)).start()

    to_mate.start()
    send_rows(t_ref, 8 * zh, (zh * 2 + c) * 16 + yx)

    @pl.when(away == 0)
    def _():
        arrived(0, (1, -1))

    @pl.when(away == 1)
    def _():
        arrived(3, (3, 1, -1))
        arrived(-3, (-3, -1, 1))

    to_mate.wait_recv()
    send_rows(mate_ref, 0, ((1 - zh) * 2 + c) * 16 + yx)

    @pl.when(away == 0)
    def _():
        arrived(6, (2, 1, -1))
        arrived(-6, (-1, 1))
        for off in (2, -2, 4, -4, 8):
            arrived(off)

    @pl.when(away == 1)
    def _():
        for off in (1, -1, 5, -5, 7, -7):
            arrived(off)

    drain(rows_ref, row_recv.at[0])
    split_rows(rows_ref, ag, ax)
    drain(piv_ref.at[pl.ds(0, 8)], sib_recv.at[0])
    block(piv_ref, part_ref, ag, ax, bg, bx, gg, xx, yx)

    slot = c * 16 + yx

    for yx2, c2 in plane_peers(yx, c):
        remote(part_ref, parts.at[slot], send1.at[0], recv1.at[0], dev(k, yx2, zh, c2)).start()

    pltpu.make_async_copy(part_ref, parts.at[slot], recv1.at[0]).start()
    drain(parts, recv1.at[0])
    for c2 in range(2):
        plane_rows[pl.ds(c2 * 8, 8), :] = jnp.sum(parts[pl.ds(c2 * 16, 16)], axis=0)

    @pl.when(zh == 0)
    def _():
        @pl.loop(1, 16)
        def _(i):
            remote(plane_rows, out_ref.at[k], send2.at[0], recv2.at[0], z_dev(z + far_first(i), yx, c)).start()

        pltpu.make_async_copy(plane_rows, out_ref.at[k], recv2.at[0]).start()

    @pl.when(zh == 1)
    def _():
        remote(plane_rows, out_ref.at[8], send2.at[0], recv3.at[0], mate_dev).start()
        pltpu.make_async_copy(plane_rows, out_ref.at[8], recv3.at[0]).start()

    to_mate.wait_send()

    @pl.when(away == 0)
    def _():
        drain(rows_ref.at[pl.ds(0, 5)], piv_send.at[0])
        drain(rows_ref.at[pl.ds(0, 3), pl.ds(0, 1)], piv_send.at[0])
        drain(piv_ref.at[pl.ds(0, 7)], hop_send.at[0])

    @pl.when(away == 1)
    def _():
        drain(rows_ref.at[pl.ds(0, 6)], piv_send.at[0])
        drain(piv_ref.at[pl.ds(0, 6)], hop_send.at[0])

    drain(rows_ref.at[pl.ds(0, 62)], row_send.at[0])
    drain(piv_ref.at[pl.ds(0, 8)], sib_send.at[0])
    drain(out_ref.at[pl.ds(0, 8)], recv2.at[0])
    drain(out_ref.at[8], recv3.at[0])
    factor(out_ref, ridge_ref, both_ref.at[0], both_ref.at[1], f_ref, k)
    drain(parts.at[pl.ds(0, 31)], send1.at[0])

    @pl.when(zh == 0)
    def _():
        drain(parts.at[pl.ds(0, 30)], send2.at[0])

    @pl.when(zh == 1)
    def _():
        drain(plane_rows, send2.at[0])


def panel(order, x, g, ridge):
    dma = pltpu.SemaphoreType.DMA
    return pl.pallas_call(
        panel_kernel,
        out_shape=jax.ShapeDtypeStruct((2, 32, 128), F32),
        in_specs=[HBM] * 4,
        out_specs=VM,
        scratch_shapes=[
            pltpu.VMEM((9, 16, 128), F32),
            pltpu.VMEM((128, 128), F32),
            pltpu.VMEM((1, 128), F32),
            pltpu.SMEM((1, 32), jnp.int32),
            pltpu.VMEM((49, 8, 32), BF16),
            pltpu.VMEM((32, 8, 49), BF16),
            pltpu.VMEM((128, 49), F32),
            pltpu.VMEM((128, 49), F32),
            pltpu.VMEM((16, 8, 128), F32),
            pltpu.VMEM((16, 16, 128), BF16),
            pltpu.VMEM((8, 16, 128), BF16),
            pltpu.VMEM((64, 4, 16, 128), BF16),
            pltpu.VMEM((16, 16, 16, 128), BF16),
        ]
        + [pltpu.VMEM((512, 512), BF16)] * 4
        + [pltpu.VMEM((512, 512), F32)] * 2
        + [pltpu.VMEM((8, 128), F32), pltpu.VMEM((32, 8, 128), F32), pltpu.VMEM((16, 128), F32)]
        + [dma((n,)) for n in (2, 1, 1, 1, 16, 1, 4, 1, 1, 1, 1, 1, 1, 1)],
        compiler_params=pltpu.CompilerParams(
            collective_id=0, has_side_effects=True, vmem_limit_bytes=56 * 1024 * 1024),
        name="panel",
    )(order, x, g, ridge)


def local(activations, cotangents, ordering, ridge):
    x = activations.transpose(1, 2, 3, 0).reshape(49, 8, 32)
    both = panel(ordering, x, cotangents, ridge.reshape(1, 128))
    return both[0], both[1]


def solution(mesh):
    return jax.shard_map(
        local,
        mesh=mesh,
        in_specs=(P("rows", None, None, "chan"), P("rows", "chan", None), P("rows", None), P()),
        out_specs=(P("rows", None), P("rows", None)),
        check_vma=False,
    )
```

```python
import jax
import jax.numpy as jnp
from jax import lax
from jax.experimental import pallas as pl
from jax.experimental.pallas import tpu as pltpu
from jax.sharding import PartitionSpec as P

F32 = jnp.float32
BF16 = jnp.bfloat16
MESH = pl.DeviceIdType.MESH
VM = pl.BlockSpec(memory_space=pltpu.VMEM)
HBM = pl.BlockSpec(memory_space=pltpu.HBM)


def place():
    k = lax.axis_index("rows")
    j = lax.axis_index("chan")
    return k, j // 4, (j // 2) % 2, j % 2


def dev(k, yx, zh, c):
    return {"rows": k, "chan": (yx * 2 + zh) * 2 + c}


def plane_peers(yx, c):
    steps = sorted(((dy, dx) for dy in range(4) for dx in range(4)),
                   key=lambda step: -sum(min(d, 4 - d) for d in step))
    for dy, dx in steps:
        for flip in (0, 1):
            if dy or dx or flip:
                yield ((yx // 4 + dy) % 4) * 4 + (yx + dx) % 4, (c + flip) % 2


def far_first(i):
    return 8 + (i // 2) * (1 - 2 * (i % 2))


def z_dev(z, yx, c):
    z = z % 16
    return dev(z % 8, yx, z // 8, c)


def lay_out(order_ref, x_ref, g_ref, out_ref, ge, go, xs, c):
    pos = lax.broadcasted_iota(jnp.int32, (49, 128), 0)
    lane = lax.broadcasted_iota(jnp.int32, (49, 128), 1)
    slot = (pos // 7) * 8 + pos % 7
    low = jnp.where(lane == slot, 1.0, 0.0).astype(BF16)
    high = jnp.where(lane == slot + 64, 1.0, 0.0).astype(BF16)
    for u in range(16):
        ge[pl.ds(u * 8, 8), :] = g_ref[order_ref[0, 2 * u]].astype(F32)
        go[pl.ds(u * 8, 8), :] = g_ref[order_ref[0, 2 * u + 1]].astype(F32)
    grads = jnp.dot(ge[...].astype(BF16), low, preferred_element_type=F32) + jnp.dot(
        go[...].astype(BF16), high, preferred_element_type=F32
    )
    grads = grads.reshape(16, 8, 128)
    unit = lax.broadcasted_iota(jnp.int32, (16, 32), 0)
    example = lax.broadcasted_iota(jnp.int32, (16, 32), 1)
    even = jnp.zeros((16, 32), F32)
    odd = jnp.zeros((16, 32), F32)
    for u in range(16):
        even = jnp.where((unit == u) & (example == order_ref[0, 2 * u]), 1.0, even)
        odd = jnp.where((unit == u) & (example == order_ref[0, 2 * u + 1]), 1.0, odd)
    even = even.astype(BF16)
    odd = odd.astype(BF16)
    for ch in range(8):
        part = x_ref[:, ch, :]
        dims = (((0,), (0,)), ((), ()))
        at_low = lax.dot_general(part, low, dims, preferred_element_type=F32).astype(BF16)
        at_high = lax.dot_general(part, high, dims, preferred_element_type=F32).astype(BF16)
        xs[:, ch, :] = jnp.dot(even, at_low, preferred_element_type=F32) + jnp.dot(
            odd, at_high, preferred_element_type=F32
        )
    inputs = xs[...]
    first = jnp.where(c == 0, grads, inputs)
    second = jnp.where(c == 0, inputs, grads)
    out_ref[...] = jnp.concatenate([first, second], axis=1).astype(BF16)


def split(z2, u, even, odd, grads, inputs):
    mask = lax.broadcasted_iota(jnp.int32, (16, 16, 128), 1) < 8
    at = pl.ds(z2 * 256, 256), pl.ds(u * 128, 128)
    grads[at] = jnp.where(mask, even, odd).reshape(256, 128)
    inputs[at] = jnp.where(mask, odd, even).reshape(256, 128)


def split_rows(rows_ref, ag, ax):
    for z2 in range(2):
        for u in range(4):
            split(z2, u, rows_ref[pl.ds(z2 * 32, 16), u], rows_ref[pl.ds(z2 * 32 + 16, 16), u], ag, ax)


def block(piv_ref, out_ref, ag, ax, bg, bx, gg, xx, yx):
    dims = (((0,), (0,)), ((), ()))
    for pair in range(2):
        for u in (2 * pair, 2 * pair + 1):
            for z2 in range(2):
                chunk = (u * 2 + z2) * 2
                split(z2, u, piv_ref[chunk], piv_ref[chunk + 1], bg, bx)
        at = slice(None), pl.ds(pair * 256, 256)
        gg[at] = lax.dot_general(ag[...], bg[at], dims, preferred_element_type=F32)
        xx[at] = lax.dot_general(ax[...], bx[at], dims, preferred_element_type=F32)
    lanes = lax.broadcasted_iota(jnp.int32, (128, 128), 0)
    cols = lax.broadcasted_iota(jnp.int32, (128, 128), 1)
    piv0 = 16 * (yx % 2) + 2 * ((yx // 4) * 2 + (yx % 4) // 2)
    pieces = jnp.zeros((8, 128), F32)
    for t in range(4):
        col = pl.ds(t * 128, 128)
        summed = []
        for e in range(8):
            wide = xx[pl.ds(e * 64, 64), col]
            wide = (
                wide
                + pltpu.roll(pltpu.roll(wide, 1, 0), 1, 1)
                + pltpu.roll(pltpu.roll(wide, 63, 0), 127, 1)
            )
            wide = (
                wide
                + pltpu.roll(pltpu.roll(wide, 8, 0), 8, 1)
                + pltpu.roll(pltpu.roll(wide, 56, 0), 120, 1)
            )
            summed.append(jnp.sum(gg[pl.ds(e * 64, 64), col] * wide, axis=0, keepdims=True))
        folded = jnp.concatenate(summed, axis=0)
        spread = jnp.where(cols == piv0 + 32 * t + lanes // 64, 1.0, 0.0)
        pieces = pieces + jnp.dot(folded, spread, precision=lax.Precision.HIGHEST, preferred_element_type=F32)
    out_ref[...] = pieces


def eliminate(left, right, store):
    full = (8, 128)
    for m0 in range(16):
        j0 = 8 * m0
        rows = [jnp.broadcast_to(left[m0][i:i + 1, :], full) for i in range(8)]
        rights = [jnp.broadcast_to(right[m0][i:i + 1, :], full) for i in range(8)]
        cols = [jnp.broadcast_to(left[m0][:, j0 + l:j0 + l + 1], full) for l in range(8)]
        e = [[jnp.broadcast_to(cols[l][i:i + 1, :], full) if i <= l else None for l in range(8)] for i in range(8)]
        inverse, ratio = [], {}
        for i in range(8):
            if i % 2 == 0:
                inverse.append(1.0 / e[i][i])
                inverse.append(e[i][i] / (e[i][i] * e[i + 1][i + 1] - e[i][i + 1] * e[i][i + 1]))
            for l in range(i + 1, 8):
                ratio[i, l] = e[i][l] * inverse[i]
            for l in range(i + 1, 8):
                for n in range(l, 8):
                    e[l][n] = e[l][n] - ratio[i, l] * e[i][n]
                rows[l] = rows[l] - ratio[i, l] * rows[i]
                rights[l] = rights[l] - ratio[i, l] * rights[i]
        for i in range(8):
            store(j0 + i, rights[i] * lax.rsqrt(e[i][i]))
        if m0 == 15:
            break
        for i in reversed(range(8)):
            rows[i] = rows[i] * inverse[i]
            rights[i] = rights[i] * inverse[i]
            for l in reversed(range(i + 1, 8)):
                rows[i] = rows[i] - ratio[i, l] * rows[l]
                rights[i] = rights[i] - ratio[i, l] * rights[l]
        for m in range(m0 + 1, 16):
            factors = [jnp.broadcast_to(left[m][:, j0 + i:j0 + i + 1], full) for i in range(8)]
            for side, vectors in ((left, rows), (right, rights)):
                terms = [f * v for f, v in zip(factors, vectors)]
                while len(terms) > 1:
                    terms = [terms[n] + terms[n + 1] for n in range(0, len(terms), 2)]
                side[m] = side[m] - terms[0]


def factor(panel_ref, ridge_ref, gram_ref, factor_ref, f_ref, k):
    gram_ref[pl.ds(0, 16), :] = panel_ref[k]
    gram_ref[pl.ds(16, 16), :] = panel_ref[8]
    gram = gram_ref[...]
    diag = panel_ref[0:8].reshape(128, 128)
    row = lax.broadcasted_iota(jnp.int32, (128, 128), 0)
    col = lax.broadcasted_iota(jnp.int32, (128, 128), 1)
    system = 0.5 * (diag + diag.T) + jnp.where(row == col, ridge_ref[...], 0.0)
    right = jnp.concatenate([gram, jnp.zeros((96, 128), F32)], axis=0).T
    left = [system[8 * m:8 * m + 8] for m in range(16)]
    right = [right[8 * m:8 * m + 8] for m in range(16)]

    def store(row, values):
        f_ref[pl.ds(row, 1), :] = values[0:1]

    eliminate(left, right, store)
    factor_ref[...] = f_ref[...].T[:32]


def panel_kernel(order_hbm, x_hbm, g_hbm, ridge_hbm, both_ref,
                 out_ref, f_ref, ridge_ref, order_ref, x_ref, g_ref, ge, go, xs, t_ref, mate_ref, rows_ref, piv_ref, ag, ax, bg, bx, gg, xx, part_ref, parts, plane_rows,
                 mate_sem, row_send, row_recv, piv_send, piv_recv, hop_send, in_sem,
                 sib_send, sib_recv, send1, recv1, send2, recv2, recv3):
    k, yx, zh, c = place()
    z = zh * 8 + k
    away = (k + yx) % 2
    mate_dev = dev(k, yx, 1 - zh, c)
    sib_dev = dev(k, yx, zh, 1 - c)

    barrier = pltpu.get_barrier_semaphore()

    def signal(target):
        pl.semaphore_signal(barrier, inc=1, device_id=target, device_id_type=MESH)

    @pl.loop(1, 16)
    def _(i):
        signal(z_dev(z + far_first(i), yx, c))

    @pl.when(away == 1)
    def _():
        @pl.loop(0, 16)
        def _(i):
            signal(z_dev(z + 3, i, c))
            signal(z_dev(z + 13, i, c))

    operands = [
        pltpu.make_async_copy(src, dst, in_sem.at[n])
        for n, (src, dst) in enumerate(((order_hbm, order_ref), (x_hbm, x_ref), (g_hbm, g_ref), (ridge_hbm, ridge_ref)))
    ]
    for copy in operands:
        copy.start()

    for yx2, c2 in plane_peers(yx, c):
        signal(dev(k, yx2, zh, c2))

    for copy in operands:
        copy.wait()
    lay_out(order_ref, x_ref, g_ref, t_ref, ge, go, xs, c)
    pl.semaphore_wait(barrier, 62)

    def remote(src, dst, send, recv, target):
        return pltpu.make_async_remote_copy(
            src_ref=src, dst_ref=dst, send_sem=send, recv_sem=recv, device_id=target, device_id_type=MESH)

    def drain(ref, sem):
        pltpu.make_async_copy(ref, ref, sem).wait()

    to_mate = remote(t_ref.at[pl.ds(8 * (1 - zh), 8)], mate_ref, mate_sem.at[0], mate_sem.at[1], mate_dev)

    def chunk_of(src_z):
        src_z = (src_z + 32) % 16
        return (((src_z % 8) // 2) * 2 + src_z // 8) * 2 + c

    own_chunk = chunk_of(z)
    for step in (3, 13, 0):
        for u in range(8):
            target = (u // 2) * 4 + 2 * (u % 2) + k % 2
            recv = piv_recv.at[{3: 3, 13: 13, 0: 0}[step]]
            tile = remote(t_ref.at[u], piv_ref.at[own_chunk, yx], piv_send.at[0], recv, z_dev(z + step, target, c))
            if step:
                tile.start()
                continue

            @pl.when(target == yx)
            def _():
                pltpu.make_async_copy(t_ref.at[u], piv_ref.at[own_chunk, yx], recv).start()

            @pl.when(target != yx)
            def _():
                tile.start()

    def send_rows(src_ref, base, slot):
        for yx2, c2 in plane_peers(yx, c):
            remote(src_ref.at[pl.ds(base + 4 * c2, 4)], rows_ref.at[slot], row_send.at[0], row_recv.at[0],
                   dev(k, yx2, zh, c2)).start()

        pltpu.make_async_copy(src_ref.at[pl.ds(base + 4 * c, 4)], rows_ref.at[slot], row_recv.at[0]).start()

    def piv_copy(chunk, target, send, recv):
        return remote(piv_ref.at[chunk], piv_ref.at[chunk], send, recv, target)

    def sib_copy(chunk):
        return piv_copy(chunk, sib_dev, sib_send.at[0], sib_recv.at[0])

    def hop(off, step):
        return piv_copy(chunk_of(z - off), z_dev(z + 16 + step, yx, c), hop_send.at[0], piv_recv.at[(off + step) % 16])

    def arrived(off, steps=()):
        drain(piv_ref.at[chunk_of(z - off)], piv_recv.at[off % 16])
        for step in steps:
            hop(off, step).start()
        sib_copy(chunk_of(z - off)).start()

    to_mate.start()
    send_rows(t_ref, 8 * zh, (zh * 2 + c) * 16 + yx)

    @pl.when(away == 0)
    def _():
        arrived(0, (1, -1))

    @pl.when(away == 1)
    def _():
        arrived(3, (3, 1, -1))
        arrived(-3, (-3, -1, 1))

    to_mate.wait_recv()
    send_rows(mate_ref, 0, ((1 - zh) * 2 + c) * 16 + yx)

    @pl.when(away == 0)
    def _():
        arrived(6, (2, 1, -1))
        arrived(-6, (-1, 1))
        for off in (2, -2, 4, -4, 8):
            arrived(off)

    @pl.when(away == 1)
    def _():
        for off in (1, -1, 5, -5, 7, -7):
            arrived(off)

    drain(rows_ref, row_recv.at[0])
    split_rows(rows_ref, ag, ax)
    drain(piv_ref.at[pl.ds(0, 8)], sib_recv.at[0])
    block(piv_ref, part_ref, ag, ax, bg, bx, gg, xx, yx)

    slot = c * 16 + yx

    for yx2, c2 in plane_peers(yx, c):
        remote(part_ref, parts.at[slot], send1.at[0], recv1.at[0], dev(k, yx2, zh, c2)).start()

    pltpu.make_async_copy(part_ref, parts.at[slot], recv1.at[0]).start()
    drain(parts, recv1.at[0])
    for c2 in range(2):
        plane_rows[pl.ds(c2 * 8, 8), :] = jnp.sum(parts[pl.ds(c2 * 16, 16)], axis=0)

    @pl.when(zh == 0)
    def _():
        @pl.loop(1, 16)
        def _(i):
            remote(plane_rows, out_ref.at[k], send2.at[0], recv2.at[0], z_dev(z + far_first(i), yx, c)).start()

        pltpu.make_async_copy(plane_rows, out_ref.at[k], recv2.at[0]).start()

    @pl.when(zh == 1)
    def _():
        remote(plane_rows, out_ref.at[8], send2.at[0], recv3.at[0], mate_dev).start()
        pltpu.make_async_copy(plane_rows, out_ref.at[8], recv3.at[0]).start()

    to_mate.wait_send()

    @pl.when(away == 0)
    def _():
        drain(rows_ref.at[pl.ds(0, 5)], piv_send.at[0])
        drain(rows_ref.at[pl.ds(0, 3), pl.ds(0, 1)], piv_send.at[0])
        drain(piv_ref.at[pl.ds(0, 7)], hop_send.at[0])

    @pl.when(away == 1)
    def _():
        drain(rows_ref.at[pl.ds(0, 6)], piv_send.at[0])
        drain(piv_ref.at[pl.ds(0, 6)], hop_send.at[0])

    drain(rows_ref.at[pl.ds(0, 62)], row_send.at[0])
    drain(piv_ref.at[pl.ds(0, 8)], sib_send.at[0])
    drain(out_ref.at[pl.ds(0, 8)], recv2.at[0])
    drain(out_ref.at[8], recv3.at[0])
    factor(out_ref, ridge_ref, both_ref.at[0], both_ref.at[1], f_ref, k)
    drain(parts.at[pl.ds(0, 31)], send1.at[0])

    @pl.when(zh == 0)
    def _():
        drain(parts.at[pl.ds(0, 30)], send2.at[0])

    @pl.when(zh == 1)
    def _():
        drain(plane_rows, send2.at[0])


def panel(order, x, g, ridge):
    dma = pltpu.SemaphoreType.DMA
    return pl.pallas_call(
        panel_kernel,
        out_shape=jax.ShapeDtypeStruct((2, 32, 128), F32),
        in_specs=[HBM] * 4,
        out_specs=VM,
        scratch_shapes=[
            pltpu.VMEM((9, 16, 128), F32),
            pltpu.VMEM((128, 128), F32),
            pltpu.VMEM((1, 128), F32),
            pltpu.SMEM((1, 32), jnp.int32),
            pltpu.VMEM((49, 8, 32), BF16),
            pltpu.VMEM((32, 8, 49), BF16),
            pltpu.VMEM((128, 49), F32),
            pltpu.VMEM((128, 49), F32),
            pltpu.VMEM((16, 8, 128), F32),
            pltpu.VMEM((16, 16, 128), BF16),
            pltpu.VMEM((8, 16, 128), BF16),
            pltpu.VMEM((64, 4, 16, 128), BF16),
            pltpu.VMEM((16, 16, 16, 128), BF16),
        ]
        + [pltpu.VMEM((512, 512), BF16)] * 4
        + [pltpu.VMEM((512, 512), F32)] * 2
        + [pltpu.VMEM((8, 128), F32), pltpu.VMEM((32, 8, 128), F32), pltpu.VMEM((16, 128), F32)]
        + [dma((n,)) for n in (2, 1, 1, 1, 16, 1, 4, 1, 1, 1, 1, 1, 1, 1)],
        compiler_params=pltpu.CompilerParams(
            collective_id=0, has_side_effects=True, vmem_limit_bytes=56 * 1024 * 1024),
        name="panel",
    )(order, x, g, ridge)


def local(activations, cotangents, ordering, ridge):
    x = activations.transpose(1, 2, 3, 0).reshape(49, 8, 32)
    both = panel(ordering, x, cotangents, ridge.reshape(1, 128))
    return both[0], both[1]


def solution(mesh):
    return jax.shard_map(
        local,
        mesh=mesh,
        in_specs=(P("rows", None, None, "chan"), P("rows", "chan", None), P("rows", None), P()),
        out_specs=(P("rows", None), P("rows", None)),
        check_vma=False,
    )
```
